128 devices in a mesh: ia: 4 (over z_lo, core), ja: 4 (over y), al: 8 (over x, z_hi).
Axes of the slice: x: 4, y: 4, z: 4 (z_hi: 2, z_lo: 2; z = z_hi * 2 + z_lo), core: 2. Of those that a mesh axis runs over, the one named last changes fastest.
Arguments:
- inputs: bfloat16 [1024, 6144], P(('ia', 'al'), 'ja'), may hold values from -6 to 6
- first_weight: bfloat16 [6144, 24576], P(('ja', 'ia'), 'al'), may hold values from -0.078125 to 0.078125
- second_weight: bfloat16 [24576, 6144], P(('al', 'ia'), 'ja'), may hold values from -0.0390625 to 0.0390625
- cotangent: bfloat16 [1024, 6144], P(('ia', 'al'), 'ja'), may hold values from -1.5 to 1.5
Outputs:
- output: bfloat16 [1024, 6144], P(('ia', 'al'), 'ja')
- input_grad: bfloat16 [1024, 6144], P(('ia', 'al'), 'ja')
- first_grad: bfloat16 [6144, 24576], P(('ja', 'ia'), 'al')
- second_grad: bfloat16 [24576, 6144], P(('al', 'ia'), 'ja')
The draws below stay inside these ranges and needn't reach their ends.
All inputs are finite; a program needn't handle non-finite values.
Results may differ from the reference program's by a relative error of at most 0.025.
Values may be sent and summed in bfloat16 or wider, within the bound.
A program may use at most 128 MiB of HBM per device.

```python
import jax
import jax.numpy as jnp
from jax import lax

D = 6144
FF = 24576
TOK_DEV = 256
TOKENS = 1024
N_IA = 4


def levels(own_key, extent, shards, least, high):
    level, own = 1.0, jax.random.fold_in(own_key, 6)
    for dim, blocks in shards:
        heights = jnp.exp(jax.random.uniform(jax.random.fold_in(own, dim), (blocks,), jnp.float32, least / len(shards), high / len(shards)))
        level = level * jnp.repeat(heights, extent[dim] // blocks).reshape([-1 if axis == dim else 1 for axis in range(len(extent))])
    return level


def gaussian(stream_key, extent, scale, limit, pieces=(), kind=jnp.bfloat16):
    array = jax.random.normal(stream_key, extent, jnp.float32) * scale
    if len(pieces) > 0:
        array = levels(stream_key, extent, pieces, -0.22, 0.18) * array
    return jnp.clip(array, min=-limit, max=limit).astype(kind)


def setup_inputs(seed: int = 0) -> dict:
    keys = jax.random.split(jax.random.key(seed), 5)
    inputs = gaussian(keys[0], (TOKENS, D), 1.0, 6.0, ((0, 32), (1, 4)))
    first_weight = gaussian(keys[1], (D, FF), D ** -0.5, 0.078125, ((0, 16), (1, 8)))
    second_weight = gaussian(keys[2], (FF, D), FF ** -0.5, 0.0390625, ((0, 32), (1, 4)))
    cotangent = gaussian(keys[3], (TOKENS, D), 0.25, 1.5, ((0, 32), (1, 4)))
    return {"inputs": inputs, "first_weight": first_weight, "second_weight": second_weight, "cotangent": cotangent}


def gelu_parts(pre):
    scaled = pre * 0.7071067811865476
    cdf = 0.5 * (1.0 + lax.erf(scaled))
    value = pre * cdf
    slope = cdf + pre * jnp.exp(-0.5 * pre * pre) * 0.3989422804014327
    return value, slope


def reference(inputs, first_weight, second_weight, cotangent):
    pre = jnp.dot(inputs, first_weight, preferred_element_type=jnp.float32)
    value, slope = gelu_parts(pre)
    activ = value.astype(jnp.bfloat16)
    output = jnp.dot(activ, second_weight, preferred_element_type=jnp.float32).astype(jnp.bfloat16)
    grad_act = lax.dot_general(cotangent, second_weight, (((1,), (1,)), ((), ())), preferred_element_type=jnp.float32)
    grad_hid = (grad_act * slope).astype(jnp.bfloat16)
    input_grad = lax.dot_general(grad_hid, first_weight, (((1,), (1,)), ((), ())), preferred_element_type=jnp.float32).astype(jnp.bfloat16)

    def add_group(carry, group):
        start = (group * TOK_DEV).astype(jnp.int32)
        in_rows = lax.dynamic_slice_in_dim(inputs, start, TOK_DEV, 0)
        hid_rows = lax.dynamic_slice_in_dim(grad_hid, start, TOK_DEV, 0)
        act_rows = lax.dynamic_slice_in_dim(activ, start, TOK_DEV, 0)
        cot_rows = lax.dynamic_slice_in_dim(cotangent, start, TOK_DEV, 0)
        term_one = lax.dot_general(in_rows, hid_rows, (((0,), (0,)), ((), ())), preferred_element_type=jnp.float32).astype(jnp.bfloat16)
        term_two = lax.dot_general(act_rows, cot_rows, (((0,), (0,)), ((), ())), preferred_element_type=jnp.float32).astype(jnp.bfloat16)
        term_one, term_two = lax.optimization_barrier((term_one, term_two))
        return (carry[0] + term_one.astype(jnp.float32), carry[1] + term_two.astype(jnp.float32)), None

    start_carry = (jnp.zeros((D, FF), jnp.float32), jnp.zeros((FF, D), jnp.float32))
    sums, unused = lax.scan(add_group, start_carry, jnp.arange(N_IA, dtype=jnp.int32))
    return output, input_grad, sums[0].astype(jnp.bfloat16), sums[1].astype(jnp.bfloat16)
```

```python
import jax
import jax.numpy as jnp
from jax import lax
from jax.sharding import PartitionSpec as P


def gelu_parts(pre):
    scaled = pre * 0.7071067811865476
    cdf = 0.5 * (1.0 + lax.erf(scaled))
    value = pre * cdf
    slope = cdf + pre * jnp.exp(-0.5 * pre * pre) * 0.3989422804014327
    return (value, slope)


def shards(inputs, first_weight, second_weight, cotangent):
    bf16, f32 = jnp.bfloat16, jnp.float32
    mine = lax.all_to_all(inputs, "ia", split_axis=1, concat_axis=0, tiled=True)
    tokens = lax.all_gather(mine, "al", axis=0, tiled=True)
    pre = jnp.dot(tokens, first_weight, preferred_element_type=f32).astype(bf16)
    pre = lax.psum_scatter(pre, "ia", scatter_dimension=1, tiled=True)
    pre = lax.psum_scatter(pre, "ja", scatter_dimension=0, tiled=True).astype(f32)
    cot = lax.all_gather(cotangent, ("al", "ia"), axis=0, tiled=True)
    grad_act = lax.dot_general(
        cot, second_weight, (((1,), (1,)), ((), ())), preferred_element_type=f32
    ).astype(bf16)
    grad_act = lax.psum_scatter(grad_act, "ja", scatter_dimension=0, tiled=True).astype(f32)
    value, slope = gelu_parts(pre)
    grad_hid = (grad_act * slope).astype(bf16)
    grad_hid = lax.all_gather(grad_hid, "ia", axis=1, tiled=True)
    grad_hid = lax.all_gather(grad_hid, "ja", axis=0, tiled=True)
    activ = lax.all_gather(value.astype(bf16), "ja", axis=0, tiled=True)
    output = jnp.dot(activ, second_weight, preferred_element_type=f32).astype(bf16)
    output = lax.psum_scatter(output, ("al", "ia"), scatter_dimension=0, tiled=True)
    second_grad = lax.dot_general(
        activ, cot, (((0,), (0,)), ((), ())), preferred_element_type=f32
    ).astype(bf16)
    input_grad = lax.dot_general(
        grad_hid, first_weight, (((1,), (1,)), ((), ())), preferred_element_type=f32
    ).astype(bf16)
    input_grad = lax.psum_scatter(input_grad, "al", scatter_dimension=0, tiled=True)
    input_grad = lax.all_to_all(input_grad, "ia", split_axis=0, concat_axis=1, tiled=True)
    first_grad = lax.dot_general(
        tokens, grad_hid, (((0,), (0,)), ((), ())), preferred_element_type=f32
    ).astype(bf16)
    return (output, input_grad, first_grad, second_grad)


def solution(mesh):
    in_specs = (
        P(("ia", "al"), "ja"),
        P(("ja", "ia"), "al"),
        P(("al", "ia"), "ja"),
        P(("ia", "al"), "ja"),
    )
    out_specs = (
        P(("ia", "al"), "ja"),
        P(("ia", "al"), "ja"),
        P(("ja", "ia"), "al"),
        P(("al", "ia"), "ja"),
    )
    return jax.shard_map(shards, mesh=mesh, in_specs=in_specs, out_specs=out_specs, check_vma=False)
```

```python
import jax
import jax.numpy as jnp
from jax import lax
from jax.experimental import pallas as pl
from jax.experimental.pallas import tpu as pltpu
from jax.sharding import PartitionSpec as P

BF16, F32 = jnp.bfloat16, jnp.float32
MESH = pl.DeviceIdType.MESH
NT = (((1,), (1,)), ((), ()))


def gelu_parts(pre):
    scaled = pre * 0.7071067811865476
    cdf = 0.5 * (1.0 + lax.erf(scaled))
    value = pre * cdf
    slope = cdf + pre * jnp.exp(-0.5 * pre * pre) * 0.3989422804014327
    return (value, slope)


MESSAGES = {}


def number(name, count):
    MESSAGES[name] = sum(size for _, size in LAYOUT[:[n for n, _ in LAYOUT].index(name)])
    return count


LAYOUT = [
    ("xz", 3), ("xx", 3), ("cz", 3), ("cx", 3), ("w1", 1), ("w2", 1),
    ("pa", 8), ("pb", 8), ("pc", 8), ("pz", 4),
    ("ga", 8), ("gb", 8), ("gc", 8),
    ("as", 8), ("af", 8), ("hz", 4), ("hs", 16), ("hf", 16),
    ("ox", 3), ("oz", 3), ("ix", 3), ("iz", 3), ("sg", 1), ("fg", 2),
]
for _name, _count in LAYOUT:
    number(_name, _count)
N_MESSAGES = sum(size for _, size in LAYOUT)


def kernel(
    x_ref, w1_ref, w2_ref, cot_ref,
    out_ref, ig_ref, fg_ref, sg_ref,
    w1, w2, xg, xgt, cotg,
    p, pa, pb, pc, ps, pr,
    g, ga, gb, gc,
    slope, act, actt, gh,
    o, orx, osum, orz, ofin,
    ig, irx, isum, irz, ifin,
    sgs, sgr, sgo, fgs, fgr, fgo,
    send_sem, recv_sem, local_sem,
):
    ia, y, al = lax.axis_index("ia"), lax.axis_index("ja"), lax.axis_index("al")
    x, z, zl, c = al // 2, lax.rem(al, 2) * 2 + ia // 2, ia // 2, lax.rem(ia, 2)

    def at_x(d):
        return (ia, y, lax.rem(x + d + 4, 4) * 2 + lax.rem(al, 2))

    def at_y(d):
        return (ia, lax.rem(y + d + 4, 4), al)

    def at_z(d):
        other = lax.rem(z + d + 4, 4)
        return (lax.rem(other, 2) * 2 + c, y, x * 2 + other // 2)

    core = (zl * 2 + 1 - c, y, al)
    pair = ((1 - zl) * 2 + c, y, al)
    y1, y2, y3 = lax.rem(y + 1, 4), lax.rem(y + 2, 4), lax.rem(y + 3, 4)

    barrier = pltpu.get_barrier_semaphore()
    partners = [at_x(1), at_x(2), at_x(3), at_y(1), at_y(3), at_z(1), at_z(2), at_z(3), core]
    for partner in partners:
        pl.semaphore_signal(barrier, inc=1, device_id=partner, device_id_type=MESH)

    sent = {}

    def copy(name, k, src, dst, device):
        i = MESSAGES[name] + k
        made = pltpu.make_async_remote_copy(
            src_ref=src, dst_ref=dst, send_sem=send_sem.at[i], recv_sem=recv_sem.at[i],
            device_id=device, device_id_type=MESH,
        )
        made.start()
        sent[(name, k)] = made

    def arrived(name, k):
        sent[(name, k)].wait_recv()

    n_local = [0]

    def local(src, dst):
        made = pltpu.make_async_copy(src, dst, local_sem.at[n_local[0]])
        made.start()
        n_local[0] += 1
        return made

    own_half = pl.ds(pl.multiple_of(zl * 768, 768), 768)
    other_half = pl.ds(pl.multiple_of((1 - zl) * 768, 768), 768)
    w1_rows = pl.ds(pl.multiple_of(c * 384, 384), 384)
    w2_rows = pl.ds(pl.multiple_of(c * 768, 768), 768)
    load_x = local(x_ref.at[:, own_half], xg.at[0, z])
    load_w1 = local(w1_ref, w1.at[w1_rows])
    load_cot = local(cot_ref, cotg.at[0, z])
    load_w2 = local(w2_ref, w2.at[w2_rows])

    pl.semaphore_wait(barrier, len(partners))

    copy("xz", 0, x_ref.at[:, other_half], xg.at[0, z], at_z(1))
    copy("xz", 2, x_ref.at[:, other_half], xg.at[0, z], at_z(3))
    copy("xz", 1, x_ref.at[:, own_half], xg.at[0, z], at_z(2))
    copy("w1", 0, w1_ref, w1.at[w1_rows], core)
    for d in (1, 3, 2):
        copy("cz", d - 1, cot_ref, cotg.at[0, z], at_z(d))
    copy("w2", 0, w2_ref, w2.at[w2_rows], core)

    load_x.wait()
    for k in range(3):
        arrived("xz", k)
    for d in (1, 3, 2):
        copy("xx", d - 1, xg.at[0], xg.at[4 - d], at_x(d))
    load_w1.wait()
    arrived("w1", 0)

    def rows(block, half):
        return pl.ds(pl.multiple_of(block * 32 + half * 16, 16), 16)

    def pre_product(r):
        lhs = xg[r].reshape(128, 768)

        @pl.loop(0, 4)
        def _(t):
            cols = pl.ds(pl.multiple_of(t * 768, 768), 768)
            inner = pl.ds(pl.multiple_of(lax.rem(t, 2) * 768, 768), 768)
            p[r, t // 2, :, inner] = jnp.dot(lhs, w1[:, cols], preferred_element_type=F32).astype(BF16)

        copy("pa", 2 * r, p.at[r, :, rows(y2, 0)], pa.at[r, 0], at_y(3))
        copy("pa", 2 * r + 1, p.at[r, :, rows(y2, 1)], pa.at[r, 1], at_y(1))
        copy("pb", 2 * r, p.at[r, :, rows(y3, 1)], pb.at[r, 0], at_y(3))
        copy("pb", 2 * r + 1, p.at[r, :, rows(y1, 0)], pb.at[r, 1], at_y(1))

    def pre_forward(r):
        for side, (block, half, device) in enumerate(((y3, 0, at_y(3)), (y1, 1, at_y(1)))):
            arrived("pa", 2 * r + side)
            spot = rows(block, half)
            p[r, :, spot] = (p[r, :, spot].astype(F32) + pa[r, side].astype(F32)).astype(BF16)
            copy("pc", 2 * r + side, p.at[r, :, spot], pc.at[r, side], device)

    def pre_block(r, hidden):
        low = p[r, hidden, rows(y, 0)].astype(F32) + pb[r, 1, hidden].astype(F32) + pc[r, 0, hidden].astype(F32)
        high = p[r, hidden, rows(y, 1)].astype(F32) + pb[r, 0, hidden].astype(F32) + pc[r, 1, hidden].astype(F32)
        return jnp.concatenate([low, high], axis=0)

    def pre_sum(r):
        for side in range(2):
            arrived("pb", 2 * r + side)
            arrived("pc", 2 * r + side)
        ps[r] = pre_block(r, 1 - zl).astype(BF16)
        copy("pz", r, ps.at[r], pr.at[r], pair)

    def act_send(r):
        own = act.at[r, y]
        copy("as", 2 * r, own, own, at_y(3))
        copy("as", 2 * r + 1, own, own, at_y(1))

    def gelu(r):
        arrived("pz", r)
        value, slope[r] = gelu_parts(pre_block(r, zl) + pr[r].astype(F32))
        act[r, y] = value.astype(BF16)
        act_send(r)

    def act_forward(r):
        arrived("as", 2 * r)
        low = act.at[r, y1, pl.ds(0, 16)]
        copy("af", 2 * r, low, low, at_y(3))
        arrived("as", 2 * r + 1)
        high = act.at[r, y3, pl.ds(16, 16)]
        copy("af", 2 * r + 1, high, high, at_y(1))

    def grad_product(r):
        lhs = cotg[r].reshape(128, 1536)

        @pl.loop(0, 3)
        def _(t):
            cols = pl.ds(pl.multiple_of(t * 512, 512), 512)
            g[r, :, cols] = lax.dot_general(lhs, w2[cols, :], NT, preferred_element_type=F32).astype(BF16)

        copy("ga", 2 * r, g.at[r, rows(y2, 0)], ga.at[r, 0], at_y(3))
        copy("ga", 2 * r + 1, g.at[r, rows(y2, 1)], ga.at[r, 1], at_y(1))
        copy("gb", 2 * r, g.at[r, rows(y3, 1)], gb.at[r, 0], at_y(3))
        copy("gb", 2 * r + 1, g.at[r, rows(y1, 0)], gb.at[r, 1], at_y(1))

    def grad_forward(r):
        for side, (block, half, device) in enumerate(((y3, 0, at_y(3)), (y1, 1, at_y(1)))):
            arrived("ga", 2 * r + side)
            spot = rows(block, half)
            g[r, spot] = (g[r, spot].astype(F32) + ga[r, side].astype(F32)).astype(BF16)
            copy("gc", 2 * r + side, g.at[r, spot], gc.at[r, side], device)

    def hid_send(r, hidden, which):
        own = gh.at[r, hidden, y]
        copy("hs", 4 * r + 2 * which, own, own, at_y(3))
        copy("hs", 4 * r + 2 * which + 1, own, own, at_y(1))

    def hidden_grad(r):
        for side in range(2):
            arrived("gb", 2 * r + side)
            arrived("gc", 2 * r + side)
        low = g[r, rows(y, 0)].astype(F32) + gb[r, 1].astype(F32) + gc[r, 0].astype(F32)
        high = g[r, rows(y, 1)].astype(F32) + gb[r, 0].astype(F32) + gc[r, 1].astype(F32)
        gh[r, zl, y] = (jnp.concatenate([low, high], axis=0) * slope[r]).astype(BF16)
        own = gh.at[r, zl, y]
        copy("hz", r, own, own, pair)
        hid_send(r, zl, 0)

    def hidden_pair(r):
        arrived("hz", r)
        hid_send(r, 1 - zl, 1)

    def hid_forward(r, which):
        hidden = zl if which == 0 else 1 - zl
        k = 4 * r + 2 * which
        arrived("hs", k)
        low = gh.at[r, hidden, y1, pl.ds(0, 16)]
        copy("hf", k, low, low, at_y(3))
        arrived("hs", k + 1)
        high = gh.at[r, hidden, y3, pl.ds(16, 16)]
        copy("hf", k + 1, high, high, at_y(1))

    def out_product(r):
        arrived("af", 2 * r)
        arrived("af", 2 * r + 1)
        lhs = act[r].reshape(128, 1536)

        @pl.loop(0, 3)
        def _(t):
            cols = pl.ds(pl.multiple_of(t * 512, 512), 512)
            o[r, :, cols] = jnp.dot(lhs, w2[:, cols], preferred_element_type=F32).astype(BF16)

        if r:
            copy("ox", r - 1, o.at[r], orx.at[r - 1], at_x(r))

    def out_sum():
        for r in range(1, 4):
            arrived("ox", r - 1)
        total = o[0].astype(F32) + orx[0].astype(F32) + orx[1].astype(F32) + orx[2].astype(F32)
        osum[...] = total.astype(BF16).reshape(4, 32, 1536)
        for d in range(1, 4):
            copy("oz", d - 1, osum.at[lax.rem(z + d, 4)], orz.at[d - 1], at_z(d))

    def out_final():
        for d in range(1, 4):
            arrived("oz", d - 1)
        total = osum[z].astype(F32) + orz[0].astype(F32) + orz[1].astype(F32) + orz[2].astype(F32)
        ofin[...] = total.astype(BF16)
        return local(ofin, out_ref)

    def second_grad():
        for r in range(4):
            actt[:, pl.ds(r * 128, 128)] = act[r].reshape(128, 1536).T
        rhs = cotg[...].reshape(512, 1536)
        base = (1 - c) * 768

        @pl.loop(0, 3)
        def _(t):
            some = pl.ds(pl.multiple_of(base + t * 256, 256), 256)
            sgs[pl.ds(pl.multiple_of(t * 256, 256), 256)] = jnp.dot(
                actt[some], rhs, preferred_element_type=F32
            ).astype(BF16)

        copy("sg", 0, sgs, sgr, core)

    def second_grad_own():
        arrived("sg", 0)
        rhs = cotg[...].reshape(512, 1536)

        @pl.loop(0, 3)
        def _(t):
            some = pl.ds(pl.multiple_of(c * 768 + t * 256, 256), 256)
            inner = pl.ds(pl.multiple_of(t * 256, 256), 256)
            total = jnp.dot(actt[some], rhs, preferred_element_type=F32) + sgr[inner].astype(F32)
            sgo[inner] = total.astype(BF16)

        return local(sgo, sg_ref)

    def in_product(r):
        for k in range(4):
            arrived("hf", 4 * r + k)
        first = gh[r, 0].reshape(128, 1536)
        second = gh[r, 1].reshape(128, 1536)

        @pl.loop(0, 3)
        def _(t):
            some = pl.ds(pl.multiple_of(t * 256, 256), 256)
            total = lax.dot_general(first, w1[some, pl.ds(0, 1536)], NT, preferred_element_type=F32)
            total += lax.dot_general(second, w1[some, pl.ds(1536, 1536)], NT, preferred_element_type=F32)
            ig[r, :, some] = total.astype(BF16)

        if r:
            copy("ix", r - 1, ig.at[r], irx.at[r - 1], at_x(r))

    def in_sum():
        for r in range(1, 4):
            arrived("ix", r - 1)
        total = ig[0].astype(F32) + irx[0].astype(F32) + irx[1].astype(F32) + irx[2].astype(F32)
        isum[...] = total.astype(BF16).reshape(4, 32, 768)
        for d in range(1, 4):
            copy("iz", d - 1, isum.at[lax.rem(z + d, 4)], irz.at[d - 1], at_z(d))

    def in_final():
        for d in range(1, 4):
            arrived("iz", d - 1)
        ifin[0] = (isum[z].astype(F32) + irz[1].astype(F32)).astype(BF16)
        ifin[1] = (irz[0].astype(F32) + irz[2].astype(F32)).astype(BF16)
        return [local(ifin.at[0], ig_ref.at[:, own_half]), local(ifin.at[1], ig_ref.at[:, other_half])]

    def transpose_in():
        for r in range(4):
            xgt[:, pl.ds(r * 128, 128)] = xg[r].reshape(128, 768).T

    def first_grad(half):
        lhs = xgt[pl.ds(pl.multiple_of((1 - c) * 384, 128), 384)]
        rhs = gh.at[:, half]

        @pl.loop(0, 3)
        def _(t):
            cols = pl.ds(pl.multiple_of(t * 512, 512), 512)
            some = gh[:, half, :, :, cols].reshape(512, 512)
            fgs[half, :, cols] = jnp.dot(lhs, some, preferred_element_type=F32).astype(BF16)

        copy("fg", half, fgs.at[half], fgr.at[half], core)

    def first_grad_own(half):
        arrived("fg", half)
        lhs = xgt[pl.ds(pl.multiple_of(c * 384, 128), 384)]

        @pl.loop(0, 3)
        def _(t):
            cols = pl.ds(pl.multiple_of(t * 512, 512), 512)
            some = gh[:, half, :, :, cols].reshape(512, 512)
            total = jnp.dot(lhs, some, preferred_element_type=F32) + fgr[half, :, cols].astype(F32)
            fgo[half, :, cols] = total.astype(BF16)

        return local(fgo.at[half], fg_ref.at[:, pl.ds(half * 1536, 1536)])

    pre_product(0)
    load_cot.wait()
    for k in range(3):
        arrived("cz", k)
    for d in (1, 3, 2):
        copy("cx", d - 1, cotg.at[0], cotg.at[4 - d], at_x(d))
    load_w2.wait()
    arrived("w2", 0)
    arrived("xx", 2)
    pre_product(1)
    pre_forward(0)
    arrived("xx", 0)
    pre_product(3)
    pre_forward(1)
    arrived("xx", 1)
    pre_product(2)
    pre_forward(3)
    pre_sum(0)
    transpose_in()
    pre_forward(2)
    arrived("cx", 2)
    grad_product(1)
    pre_sum(1)
    arrived("cx", 0)
    grad_product(3)
    gelu(0)
    pre_sum(3)
    grad_forward(1)
    arrived("cx", 1)
    grad_product(2)
    gelu(1)
    pre_sum(2)
    grad_forward(3)
    grad_product(0)
    gelu(3)
    hidden_grad(1)
    grad_forward(2)
    act_forward(0)
    gelu(2)
    hidden_grad(3)
    grad_forward(0)
    act_forward(1)
    hidden_pair(1)
    hidden_pair(3)
    hidden_grad(2)
    act_forward(3)
    hid_forward(1, 0)
    hidden_grad(0)
    act_forward(2)
    hidden_pair(2)
    out_product(1)
    hid_forward(3, 0)
    hidden_pair(0)
    out_product(3)
    hid_forward(1, 1)
    hid_forward(3, 1)
    out_product(2)
    hid_forward(2, 0)
    out_product(0)
    in_product(1)
    hid_forward(0, 0)
    out_sum()
    in_product(3)
    hid_forward(2, 1)
    second_grad()
    hid_forward(0, 1)
    done = [out_final()]
    done.append(second_grad_own())
    in_product(2)
    in_product(0)
    in_sum()
    first_grad(0)
    first_grad(1)
    done += in_final()
    done.append(first_grad_own(0))
    done.append(first_grad_own(1))
    for made in sent.values():
        made.wait_send()
    for made in done:
        made.wait()


def shards(inputs, first_weight, second_weight, cotangent):
    def vmem(*shape, dtype=BF16):
        return pltpu.VMEM(shape, dtype)

    anywhere = pl.BlockSpec(memory_space=pl.ANY)
    return pl.pallas_call(
        kernel,
        out_shape=[
            jax.ShapeDtypeStruct((32, 1536), BF16),
            jax.ShapeDtypeStruct((32, 1536), BF16),
            jax.ShapeDtypeStruct((384, 3072), BF16),
            jax.ShapeDtypeStruct((768, 1536), BF16),
        ],
        in_specs=[anywhere] * 4,
        out_specs=[anywhere] * 4,
        scratch_shapes=[
            vmem(768, 3072), vmem(1536, 1536), vmem(4, 4, 32, 768), vmem(768, 512), vmem(4, 4, 32, 1536),
            vmem(4, 2, 128, 1536), vmem(4, 2, 2, 16, 1536), vmem(4, 2, 2, 16, 1536), vmem(4, 2, 2, 16, 1536),
            vmem(4, 32, 1536), vmem(4, 32, 1536),
            vmem(4, 128, 1536), vmem(4, 2, 16, 1536), vmem(4, 2, 16, 1536), vmem(4, 2, 16, 1536),
            vmem(4, 32, 1536, dtype=F32), vmem(4, 4, 32, 1536), vmem(1536, 512), vmem(4, 2, 4, 32, 1536),
            vmem(4, 128, 1536), vmem(3, 128, 1536), vmem(4, 32, 1536), vmem(3, 32, 1536), vmem(32, 1536),
            vmem(4, 128, 768), vmem(3, 128, 768), vmem(4, 32, 768), vmem(3, 32, 768), vmem(2, 32, 768),
            vmem(768, 1536), vmem(768, 1536), vmem(768, 1536),
            vmem(2, 384, 1536), vmem(2, 384, 1536), vmem(2, 384, 1536),
            pltpu.SemaphoreType.DMA((N_MESSAGES,)),
            pltpu.SemaphoreType.DMA((N_MESSAGES,)),
            pltpu.SemaphoreType.DMA((10,)),
        ],
        compiler_params=pltpu.CompilerParams(
            collective_id=0, has_side_effects=True, vmem_limit_bytes=60 << 20
        ),
        name="layer",
    )(inputs, first_weight, second_weight, cotangent)


def solution(mesh):
    in_specs = (
        P(("ia", "al"), "ja"),
        P(("ja", "ia"), "al"),
        P(("al", "ia"), "ja"),
        P(("ia", "al"), "ja"),
    )
    out_specs = (
        P(("ia", "al"), "ja"),
        P(("ia", "al"), "ja"),
        P(("ja", "ia"), "al"),
        P(("al", "ia"), "ja"),
    )
    return jax.shard_map(shards, mesh=mesh, in_specs=in_specs, out_specs=out_specs, check_vma=False)
```

```python
import jax
import jax.numpy as jnp
from jax import lax
from jax.experimental import pallas as pl
from jax.experimental.pallas import tpu as pltpu
from jax.sharding import PartitionSpec as P

BF16, F32 = jnp.bfloat16, jnp.float32
MESH = pl.DeviceIdType.MESH

OFFSET = (0, 2, 1, 3)
SLOT = {offset: slot for slot, offset in enumerate(OFFSET)}
PRE_CROSS = (2,)
HID_CROSS = (2, 3)


def gelu_parts(pre):
    scaled = pre * 0.7071067811865476
    cdf = 0.5 * (1.0 + lax.erf(scaled))
    value = pre * cdf
    slope = cdf + pre * jnp.exp(-0.5 * pre * pre) * 0.3989422804014327
    return (value, slope)


MESSAGES = {}


def number(name, count):
    MESSAGES[name] = sum(size for _, size in LAYOUT[:[n for n, _ in LAYOUT].index(name)])
    return count


LAYOUT = [
    ("xz", 3), ("xx", 2), ("xf", 2), ("cz", 3), ("cx", 2), ("cf", 2), ("w1", 1), ("w2", 1),
    ("pa", 8), ("pb", 8), ("pc", 8), ("pz", 4),
    ("ga", 8), ("gb", 8), ("gc", 8),
    ("as", 8), ("af", 8), ("hz", 20), ("hs", 16), ("hf", 16),
    ("ox", 3), ("oz", 3), ("ix", 3), ("iz", 3), ("sg", 1), ("fg", 2),
]
for _name, _count in LAYOUT:
    number(_name, _count)
N_MESSAGES = sum(size for _, size in LAYOUT)


def kernel(
    x_ref, w1_ref, w2_ref, cot_ref,
    out_ref, ig_ref, fg_ref, sg_ref,
    w1, w2, wt, xg, xgt, cotg,
    p, pa, pb, pc, ps, pr, prc,
    g, ga, gb, gc,
    slope, act, actt, gh,
    orx, osum, orz,
    ig, irx, isum, irz,
    gone, sgr, fgr,
    send_sem, recv_sem, local_sem,
):
    ia, y, al = lax.axis_index("ia"), lax.axis_index("ja"), lax.axis_index("al")
    x, z, zl, c = al // 2, lax.rem(al, 2) * 2 + ia // 2, ia // 2, lax.rem(ia, 2)

    def at_x(d):
        return (ia, y, lax.rem(x + d + 4, 4) * 2 + lax.rem(al, 2))

    def at_y(d):
        return (ia, lax.rem(y + d + 4, 4), al)

    def at_z(d):
        other = lax.rem(z + d + 4, 4)
        return (lax.rem(other, 2) * 2 + c, y, x * 2 + other // 2)

    core = (zl * 2 + 1 - c, y, al)
    pair = ((1 - zl) * 2 + c, y, al)
    y1, y2, y3 = lax.rem(y + 1, 4), lax.rem(y + 2, 4), lax.rem(y + 3, 4)

    barrier = pltpu.get_barrier_semaphore()
    partners = [at_x(1), at_x(2), at_x(3), at_y(1), at_y(3), at_z(1), at_z(2), at_z(3), core]
    for partner in partners:
        pl.semaphore_signal(barrier, inc=1, device_id=partner, device_id_type=MESH)

    sent = {}

    def copy(name, k, src, dst, device):
        i = MESSAGES[name] + k
        made = pltpu.make_async_remote_copy(
            src_ref=src, dst_ref=dst, send_sem=send_sem.at[i], recv_sem=recv_sem.at[i],
            device_id=device, device_id_type=MESH,
        )
        made.start()
        sent[(name, k)] = made

    def left(name, k):
        sent.pop((name, k)).wait_send()

    def arrived(name, k):
        sent[(name, k)].wait_recv()

    n_local = [0]

    def local(src, dst):
        made = pltpu.make_async_copy(src, dst, local_sem.at[n_local[0]])
        made.start()
        n_local[0] += 1
        return made

    own_half = pl.ds(pl.multiple_of(zl * 768, 768), 768)
    other_half = pl.ds(pl.multiple_of((1 - zl) * 768, 768), 768)
    w1_rows = pl.ds(pl.multiple_of(c * 384, 384), 384)
    w2_rows = pl.ds(pl.multiple_of(c * 768, 768), 768)
    load_x = local(x_ref.at[:, own_half], xg.at[0, z])
    load_w1 = local(w1_ref, w1.at[w1_rows])
    load_cot = local(cot_ref, cotg.at[0, z])
    load_w2 = local(w2_ref, w2.at[w2_rows])

    pl.semaphore_wait(barrier, len(partners))

    copy("xz", 0, x_ref.at[:, other_half], xg.at[0, z], at_z(1))
    copy("xz", 2, x_ref.at[:, other_half], xg.at[0, z], at_z(3))
    copy("xz", 1, x_ref.at[:, own_half], xg.at[0, z], at_z(2))
    copy("w1", 0, w1_ref, w1.at[w1_rows], core)
    for d in (1, 3, 2):
        copy("cz", d - 1, cot_ref, cotg.at[0, z], at_z(d))
    copy("w2", 0, w2_ref, w2.at[w2_rows], core)

    def spread(name, buffer):
        copy(name, 0, buffer.at[0], buffer.at[SLOT[1]], at_x(3))
        copy(name, 1, buffer.at[0], buffer.at[SLOT[3]], at_x(1))

    def pass_on(name, far, buffer, side):
        arrived(name, side)
        slot, half, device = ((SLOT[1], 0, at_x(3)), (SLOT[3], 2, at_x(1)))[side]
        part = pl.ds(half, 2)
        copy(far, side, buffer.at[slot, part], buffer.at[SLOT[2], part], device)

    load_x.wait()
    for k in range(3):
        arrived("xz", k)
    spread("xx", xg)
    load_w1.wait()
    arrived("w1", 0)

    def rows(block, half):
        return pl.ds(pl.multiple_of(block * 32 + half * 16, 16), 16)

    def pre_product(r):
        lhs = xg[r].reshape(128, 768)

        for half in range(2):
            cols = pl.ds(half * 1536, 1536)
            p[r, half] = jnp.dot(lhs, w1[:, cols], preferred_element_type=F32).astype(BF16)

        if r in PRE_CROSS:
            copy("pz", r, p.at[r, 1 - zl], prc.at[PRE_CROSS.index(r)], pair)
        else:
            pre_send(r)

    def pre_view(r):
        return p.at[r, pl.ds(zl, 1)] if r in PRE_CROSS else p.at[r]

    def pre_room(buffer, r, side):
        return buffer.at[r, side, pl.ds(0, 1)] if r in PRE_CROSS else buffer.at[r, side]

    def pre_send(r):
        mine = pre_view(r)
        copy("pa", 2 * r, mine.at[:, rows(y2, 0)], pre_room(pa, r, 0), at_y(3))
        copy("pa", 2 * r + 1, mine.at[:, rows(y2, 1)], pre_room(pa, r, 1), at_y(1))
        copy("pb", 2 * r, mine.at[:, rows(y3, 1)], pre_room(pb, r, 0), at_y(3))
        copy("pb", 2 * r + 1, mine.at[:, rows(y1, 0)], pre_room(pb, r, 1), at_y(1))

    def pre_cross(r):
        arrived("pz", r)

        @pl.loop(0, 4)
        def _(t):
            some = pl.ds(pl.multiple_of(t * 32, 32), 32)
            p[r, zl, some] = (p[r, zl, some].astype(F32) + prc[PRE_CROSS.index(r), some].astype(F32)).astype(BF16)

        pre_send(r)

    def pre_forward(r):
        mine = pre_view(r)
        for side, (block, half, device) in enumerate(((y3, 0, at_y(3)), (y1, 1, at_y(1)))):
            arrived("pa", 2 * r + side)
            spot = rows(block, half)
            mine[:, spot] = (mine[:, spot].astype(F32) + pre_room(pa, r, side)[...].astype(F32)).astype(BF16)
            copy("pc", 2 * r + side, mine.at[:, spot], pre_room(pc, r, side), device)

    def pre_block(r, hidden):
        k = 0 if r in PRE_CROSS else hidden
        low = p[r, hidden, rows(y, 0)].astype(F32) + pb[r, 1, k].astype(F32) + pc[r, 0, k].astype(F32)
        high = p[r, hidden, rows(y, 1)].astype(F32) + pb[r, 0, k].astype(F32) + pc[r, 1, k].astype(F32)
        return jnp.concatenate([low, high], axis=0)

    def pre_sum(r):
        for side in range(2):
            arrived("pb", 2 * r + side)
            arrived("pc", 2 * r + side)
        if r not in PRE_CROSS:
            ps[r] = pre_block(r, 1 - zl).astype(BF16)
            copy("pz", r, ps.at[r], pr.at[r], pair)

    def act_send(r):
        own = act.at[r, y]
        copy("as", 2 * r, own, own, at_y(3))
        copy("as", 2 * r + 1, own, own, at_y(1))

    def gelu(r):
        pre = pre_block(r, zl)
        if r not in PRE_CROSS:
            arrived("pz", r)
            pre += pr[r].astype(F32)
        value, slope[r] = gelu_parts(pre)
        act[r, y] = value.astype(BF16)

    def act_forward(r):
        arrived("as", 2 * r)
        low = act.at[r, y1, pl.ds(0, 16)]
        copy("af", 2 * r, low, low, at_y(3))
        arrived("as", 2 * r + 1)
        high = act.at[r, y3, pl.ds(16, 16)]
        copy("af", 2 * r + 1, high, high, at_y(1))

    def grad_product(r):
        lhs = cotg[r].reshape(128, 1536)
        for half in range(2):
            cols = pl.ds(half * 768, 768)
            g[r, :, cols] = jnp.dot(lhs, wt[half], preferred_element_type=F32).astype(BF16)

        copy("ga", 2 * r, g.at[r, rows(y2, 0)], ga.at[r, 0], at_y(3))
        copy("ga", 2 * r + 1, g.at[r, rows(y2, 1)], ga.at[r, 1], at_y(1))
        copy("gb", 2 * r, g.at[r, rows(y3, 1)], gb.at[r, 0], at_y(3))
        copy("gb", 2 * r + 1, g.at[r, rows(y1, 0)], gb.at[r, 1], at_y(1))

    def grad_forward(r):
        for side, (block, half, device) in enumerate(((y3, 0, at_y(3)), (y1, 1, at_y(1)))):
            arrived("ga", 2 * r + side)
            spot = rows(block, half)
            g[r, spot] = (g[r, spot].astype(F32) + ga[r, side].astype(F32)).astype(BF16)
            copy("gc", 2 * r + side, g.at[r, spot], gc.at[r, side], device)

    def hid_send(r, hidden, which):
        own = gh.at[r, hidden, y]
        copy("hs", 4 * r + 2 * which, own, own, at_y(3))
        copy("hs", 4 * r + 2 * which + 1, own, own, at_y(1))

    def hidden_grad(r):
        for side in range(2):
            arrived("gb", 2 * r + side)
            arrived("gc", 2 * r + side)
        low = g[r, rows(y, 0)].astype(F32) + gb[r, 1].astype(F32) + gc[r, 0].astype(F32)
        high = g[r, rows(y, 1)].astype(F32) + gb[r, 0].astype(F32) + gc[r, 1].astype(F32)
        gh[r, zl, y] = (jnp.concatenate([low, high], axis=0) * slope[r]).astype(BF16)
        own = gh.at[r, zl, y]
        hid_pair_send(r, 0, own)
        hid_send(r, zl, 0)

    def hid_pair_send(r, k, part):
        copy("hz", 5 * r + k, part, part, pair)

    def hidden_pair(r):
        arrived("hz", 5 * r)
        hid_send(r, 1 - zl, 1)

    def hid_rest(r):
        arrived("hf", 4 * r)
        hid_pair_send(r, 3, gh.at[r, zl, y2, pl.ds(0, 16)])
        arrived("hf", 4 * r + 1)
        hid_pair_send(r, 4, gh.at[r, zl, y2, pl.ds(16, 16)])

    def hid_forward(r, which):
        hidden = zl if which == 0 else 1 - zl
        k = 4 * r + 2 * which
        arrived("hs", k)
        low = gh.at[r, hidden, y1, pl.ds(0, 16)]
        copy("hf", k, low, low, at_y(3))
        arrived("hs", k + 1)
        high = gh.at[r, hidden, y3, pl.ds(16, 16)]
        copy("hf", k + 1, high, high, at_y(1))
        if r in HID_CROSS:
            hid_pair_send(r, 1, gh.at[r, hidden, y1])
            hid_pair_send(r, 2, gh.at[r, hidden, y3])

    def out_product(r):
        arrived("af", 2 * r)
        arrived("af", 2 * r + 1)
        for name in ("ga", "gb", "gc"):
            for side in range(2):
                left(name, 2 * r + side)
        lhs = act[r].reshape(128, 1536)
        g[r] = jnp.dot(lhs, w2[...], preferred_element_type=F32).astype(BF16)
        if r:
            copy("ox", r - 1, g.at[r], orx.at[r - 1], at_x(OFFSET[r]))

    def out_sum():
        for r in range(1, 4):
            arrived("ox", r - 1)
        total = g[0].astype(F32) + orx[0].astype(F32) + orx[1].astype(F32) + orx[2].astype(F32)
        osum[...] = total.astype(BF16).reshape(4, 32, 1536)
        for d in range(1, 4):
            copy("oz", d - 1, osum.at[lax.rem(z + d, 4)], orz.at[d - 1], at_z(d))

    def out_final():
        for d in range(1, 4):
            arrived("oz", d - 1)
        total = osum[z].astype(F32) + orz[0].astype(F32) + orz[1].astype(F32) + orz[2].astype(F32)
        out_ref[...] = total.astype(BF16)

    def second_part(whose):
        core_rows = pl.ds(pl.multiple_of((c if whose else 1 - c) * 768, 256), 768)
        lhs = actt[core_rows]
        for t in range(3):
            cols = pl.ds(t * 512, 512)
            rhs = cotg[:, :, :, cols].reshape(512, 512)
            total = jnp.dot(lhs, rhs, preferred_element_type=F32)
            if whose:
                sg_ref[:, cols] = (total + sgr[:, :, cols].reshape(768, 512).astype(F32)).astype(BF16)
            else:
                for part in range(2):
                    gone[part, :, cols] = total[part * 384 : part * 384 + 384].astype(BF16)

    def second_grad():
        for r in range(4):
            actt[:, pl.ds(r * 128, 128)] = act[r].reshape(128, 1536).T
        second_part(0)
        copy("sg", 0, gone, sgr, core)

    def second_grad_own():
        arrived("sg", 0)
        second_part(1)
        left("sg", 0)

    def in_product(r):
        if r in HID_CROSS:
            for k in range(5):
                arrived("hz", 5 * r + k)
        else:
            for k in range(4):
                arrived("hf", 4 * r + k)
        first = gh[r, 0].reshape(128, 1536)
        second = gh[r, 1].reshape(128, 1536)
        total = jnp.dot(first, wt[0], preferred_element_type=F32)
        total += jnp.dot(second, wt[1], preferred_element_type=F32)
        ig[r] = total.astype(BF16)
        if r:
            copy("ix", r - 1, ig.at[r], irx.at[r - 1], at_x(OFFSET[r]))

    def in_sum():
        for r in range(1, 4):
            arrived("ix", r - 1)
        total = ig[0].astype(F32) + irx[0].astype(F32) + irx[1].astype(F32) + irx[2].astype(F32)
        isum[...] = total.astype(BF16).reshape(4, 32, 768)
        for d in range(1, 4):
            copy("iz", d - 1, isum.at[lax.rem(z + d, 4)], irz.at[d - 1], at_z(d))

    def in_final():
        for d in range(1, 4):
            arrived("iz", d - 1)
        ig_ref[:, own_half] = (isum[z].astype(F32) + irz[1].astype(F32)).astype(BF16)
        ig_ref[:, other_half] = (irz[0].astype(F32) + irz[2].astype(F32)).astype(BF16)

    def transpose_in():
        for r in range(4):
            xgt[:, pl.ds(r * 128, 128)] = xg[r].reshape(128, 768).T

    def transpose_first():
        @pl.loop(0, 6)
        def _(t):
            cols = pl.ds(pl.multiple_of(t * 512, 512), 512)
            spot = pl.ds(pl.multiple_of(lax.rem(t, 3) * 512, 512), 512)
            wt[t // 3, spot] = w1[:, cols].T

    def transpose_second():
        @pl.loop(0, 6)
        def _(t):
            cols = pl.ds(pl.multiple_of(lax.rem(t, 3) * 512, 512), 512)
            some = pl.ds(pl.multiple_of(t // 3 * 768, 768), 768)
            wt[t // 3, cols] = w2[some, cols].T

    def first_grad(half, whose, early):
        core_rows = pl.ds(pl.multiple_of((c if whose else 1 - c) * 384, 128), 384)
        lhs = xgt[core_rows, pl.ds(256 if early else 0, 256)]
        slots = pl.ds(2 if early else 0, 2)
        if whose and not early:
            arrived("fg", half)

        wide = pl.ds(half * 1536, 1536)
        some = gh[slots, half].reshape(256, 1536)
        total = jnp.dot(lhs, some, preferred_element_type=F32)
        if whose:
            if not early:
                total += fg_ref[:, wide].astype(F32) + fgr[half].astype(F32)
            fg_ref[:, wide] = total.astype(BF16)
        else:
            if not early:
                total += gone[half].astype(F32)
            gone[half] = total.astype(BF16)

        if not whose and not early:
            copy("fg", half, gone.at[half], fgr.at[half], core)

    pre_product(0)
    pass_on("xx", "xf", xg, 1)
    pass_on("xx", "xf", xg, 0)
    load_cot.wait()
    for k in range(3):
        arrived("cz", k)
    spread("cx", cotg)
    pre_product(3)
    pre_product(2)
    pre_forward(0)
    arrived("xf", 0)
    arrived("xf", 1)
    pre_product(1)
    load_w2.wait()
    arrived("w2", 0)
    transpose_second()
    pre_forward(3)
    pre_forward(1)
    pre_sum(0)
    pass_on("cx", "cf", cotg, 1)
    pass_on("cx", "cf", cotg, 0)
    grad_product(3)
    grad_product(2)
    pre_cross(2)
    pre_sum(3)
    gelu(0)
    grad_forward(3)
    pre_sum(1)
    gelu(3)
    arrived("cf", 0)
    arrived("cf", 1)
    grad_product(1)
    grad_product(0)
    pre_forward(2)
    grad_forward(2)
    act_send(3)
    act_send(0)
    gelu(1)
    act_send(1)
    hidden_grad(3)
    transpose_in()
    transpose_first()
    grad_forward(1)
    pre_sum(2)
    gelu(2)
    act_send(2)
    hidden_grad(2)
    grad_forward(0)
    act_forward(3)
    act_forward(0)
    hidden_grad(1)
    act_forward(1)
    hid_forward(3, 0)
    hidden_grad(0)
    hidden_pair(1)
    act_forward(2)
    out_product(3)
    hid_forward(2, 0)
    hidden_pair(0)
    out_product(1)
    hid_rest(3)
    out_product(2)
    hid_forward(1, 0)
    hid_rest(2)
    out_product(0)
    hid_forward(0, 0)
    second_grad()
    hid_forward(1, 1)
    in_product(3)
    out_sum()
    hid_forward(0, 1)
    second_grad_own()
    in_product(2)
    for half in range(2):
        first_grad(half, 0, True)
    for half in range(2):
        first_grad(half, 1, True)
    out_final()
    in_product(1)
    in_product(0)
    in_sum()
    for half in range(2):
        first_grad(half, 0, False)
    in_final()
    for half in range(2):
        first_grad(half, 1, False)
    for made in sent.values():
        made.wait_send()


def leave(*refs):
    sems = refs[-1]
    copies = [pltpu.make_async_copy(refs[i], refs[4 + i], sems.at[i]) for i in range(4)]
    for made in copies:
        made.start()
    for made in copies:
        made.wait()


def shards(inputs, first_weight, second_weight, cotangent):
    def vmem(*shape, dtype=BF16):
        return pltpu.VMEM(shape, dtype)

    anywhere = pl.BlockSpec(memory_space=pl.ANY)
    inside = pl.BlockSpec(memory_space=pltpu.VMEM)
    shapes = [(32, 1536), (32, 1536), (384, 3072), (768, 1536)]
    results = pl.pallas_call(
        kernel,
        out_shape=[pltpu.VMEM(shape, BF16) for shape in shapes],
        in_specs=[anywhere] * 4,
        out_specs=[inside] * 4,
        scratch_shapes=[
            vmem(768, 3072), vmem(1536, 1536), vmem(2, 1536, 768), vmem(4, 4, 32, 768), vmem(768, 512), vmem(4, 4, 32, 1536),
            vmem(4, 2, 128, 1536), vmem(4, 2, 2, 16, 1536), vmem(4, 2, 2, 16, 1536), vmem(4, 2, 2, 16, 1536),
            vmem(4, 32, 1536), vmem(4, 32, 1536), vmem(len(PRE_CROSS), 128, 1536),
            vmem(4, 128, 1536), vmem(4, 2, 16, 1536), vmem(4, 2, 16, 1536), vmem(4, 2, 16, 1536),
            vmem(4, 32, 1536, dtype=F32), vmem(4, 4, 32, 1536), vmem(1536, 512), vmem(4, 2, 4, 32, 1536),
            vmem(3, 128, 1536), vmem(4, 32, 1536), vmem(3, 32, 1536),
            vmem(4, 128, 768), vmem(3, 128, 768), vmem(4, 32, 768), vmem(3, 32, 768),
            vmem(2, 384, 1536), vmem(2, 384, 1536), vmem(2, 384, 1536),
            pltpu.SemaphoreType.DMA((N_MESSAGES,)),
            pltpu.SemaphoreType.DMA((N_MESSAGES,)),
            pltpu.SemaphoreType.DMA((4,)),
        ],
        compiler_params=pltpu.CompilerParams(
            collective_id=0, has_side_effects=True, vmem_limit_bytes=50 << 20
        ),
        name="layer",
    )(inputs, first_weight, second_weight, cotangent)
    results = [pltpu.with_memory_space_constraint(result, pltpu.VMEM) for result in results]
    return pl.pallas_call(
        leave,
        out_shape=[jax.ShapeDtypeStruct(shape, BF16) for shape in shapes],
        in_specs=[inside] * 4,
        out_specs=[anywhere] * 4,
        scratch_shapes=[pltpu.SemaphoreType.DMA((4,))],
        compiler_params=pltpu.CompilerParams(vmem_limit_bytes=1 << 20),
        name="leave",
    )(*results)


def solution(mesh):
    in_specs = (
        P(("ia", "al"), "ja"),
        P(("ja", "ia"), "al"),
        P(("al", "ia"), "ja"),
        P(("ia", "al"), "ja"),
    )
    out_specs = (
        P(("ia", "al"), "ja"),
        P(("ia", "al"), "ja"),
        P(("ja", "ia"), "al"),
        P(("al", "ia"), "ja"),
    )
    return jax.shard_map(shards, mesh=mesh, in_specs=in_specs, out_specs=out_specs, check_vma=False)
```

```python
import jax
import jax.numpy as jnp
from jax import lax
from jax.experimental import pallas as pl
from jax.experimental.pallas import tpu as pltpu
from jax.sharding import PartitionSpec as P

BF16, F32 = jnp.bfloat16, jnp.float32
MESH = pl.DeviceIdType.MESH

OFFSET = (0, 2, 1, 3)
SLOT = {offset: slot for slot, offset in enumerate(OFFSET)}
PRE_CROSS = (2, 1)
HID_CROSS = (1, 3)


def gelu_parts(pre):
    scaled = pre * 0.7071067811865476
    cdf = 0.5 * (1.0 + lax.erf(scaled))
    value = pre * cdf
    slope = cdf + pre * jnp.exp(-0.5 * pre * pre) * 0.3989422804014327
    return (value, slope)


MESSAGES = {}


def number(name, count):
    MESSAGES[name] = sum(size for _, size in LAYOUT[:[n for n, _ in LAYOUT].index(name)])
    return count


LAYOUT = [
    ("xz", 3), ("xx", 2), ("xf", 2), ("cz", 3), ("cx", 2), ("cf", 2), ("w1", 1), ("w2", 1),
    ("pa", 8), ("pb", 8), ("pc", 8), ("pz", 4),
    ("ga", 8), ("gb", 8), ("gc", 8),
    ("as", 8), ("af", 8), ("hz", 20), ("hs", 16), ("hf", 16),
    ("ox", 3), ("oz", 3), ("ix", 3), ("iz", 3), ("sg", 1), ("fg", 2),
]
for _name, _count in LAYOUT:
    number(_name, _count)
N_MESSAGES = sum(size for _, size in LAYOUT)


def kernel(
    x_ref, w1_ref, w2_ref, cot_ref,
    out_ref, ig_ref, fg_ref, sg_ref,
    w1, w2, wt, xg, xgt, cotg,
    p, pa, pb, pc, ps, pr, prc,
    g, ga, gb, gc,
    slope, act, actt, gh,
    orx, osum, orz,
    ig, irx, isum, irz,
    gone, sgr, fgr,
    send_sem, recv_sem, local_sem,
):
    ia, y, al = lax.axis_index("ia"), lax.axis_index("ja"), lax.axis_index("al")
    x, z, zl, c = al // 2, lax.rem(al, 2) * 2 + ia // 2, ia // 2, lax.rem(ia, 2)

    def at_x(d):
        return (ia, y, lax.rem(x + d + 4, 4) * 2 + lax.rem(al, 2))

    def at_y(d):
        return (ia, lax.rem(y + d + 4, 4), al)

    def at_z(d):
        other = lax.rem(z + d + 4, 4)
        return (lax.rem(other, 2) * 2 + c, y, x * 2 + other // 2)

    core = (zl * 2 + 1 - c, y, al)
    pair = ((1 - zl) * 2 + c, y, al)
    y1, y2, y3 = lax.rem(y + 1, 4), lax.rem(y + 2, 4), lax.rem(y + 3, 4)

    barrier = pltpu.get_barrier_semaphore()
    partners = [at_x(1), at_x(2), at_x(3), at_y(1), at_y(3), at_z(1), at_z(2), at_z(3), core]
    for partner in partners:
        pl.semaphore_signal(barrier, inc=1, device_id=partner, device_id_type=MESH)

    sent = {}

    def copy(name, k, src, dst, device):
        i = MESSAGES[name] + k
        made = pltpu.make_async_remote_copy(
            src_ref=src, dst_ref=dst, send_sem=send_sem.at[i], recv_sem=recv_sem.at[i],
            device_id=device, device_id_type=MESH,
        )
        made.start()
        sent[(name, k)] = made

    def left(name, k):
        sent.pop((name, k)).wait_send()

    def arrived(name, k):
        sent[(name, k)].wait_recv()

    n_local = [0]

    def local(src, dst):
        made = pltpu.make_async_copy(src, dst, local_sem.at[n_local[0]])
        made.start()
        n_local[0] += 1
        return made

    own_half = pl.ds(pl.multiple_of(zl * 768, 768), 768)
    other_half = pl.ds(pl.multiple_of((1 - zl) * 768, 768), 768)
    w1_rows = pl.ds(pl.multiple_of(c * 384, 384), 384)
    w2_rows = pl.ds(pl.multiple_of(c * 768, 768), 768)
    load_x = local(x_ref.at[:, own_half], xg.at[0, z])
    load_w1 = local(w1_ref, w1.at[w1_rows])
    load_cot = local(cot_ref, cotg.at[0, z])
    load_w2 = local(w2_ref, w2.at[w2_rows])

    pl.semaphore_wait(barrier, len(partners))

    copy("xz", 0, x_ref.at[:, other_half], xg.at[0, z], at_z(1))
    copy("xz", 2, x_ref.at[:, other_half], xg.at[0, z], at_z(3))
    copy("xz", 1, x_ref.at[:, own_half], xg.at[0, z], at_z(2))
    copy("w1", 0, w1_ref, w1.at[w1_rows], core)
    for d in (1, 3, 2):
        copy("cz", d - 1, cot_ref, cotg.at[0, z], at_z(d))
    copy("w2", 0, w2_ref, w2.at[w2_rows], core)

    def spread(name, buffer):
        copy(name, 0, buffer.at[0], buffer.at[SLOT[1]], at_x(3))
        copy(name, 1, buffer.at[0], buffer.at[SLOT[3]], at_x(1))

    def pass_on(name, far, buffer, side):
        arrived(name, side)
        slot, half, device = ((SLOT[1], 0, at_x(3)), (SLOT[3], 2, at_x(1)))[side]
        part = pl.ds(half, 2)
        copy(far, side, buffer.at[slot, part], buffer.at[SLOT[2], part], device)

    load_x.wait()
    for k in range(3):
        arrived("xz", k)
    spread("xx", xg)
    load_w1.wait()
    arrived("w1", 0)

    def rows(block, half):
        return pl.ds(pl.multiple_of(block * 32 + half * 16, 16), 16)

    def pre_product(r):
        lhs = xg[r].reshape(128, 768)

        for half in range(2):
            cols = pl.ds(half * 1536, 1536)
            p[r, half] = jnp.dot(lhs, w1[:, cols], preferred_element_type=F32).astype(BF16)

        if r in PRE_CROSS:
            copy("pz", r, p.at[r, 1 - zl], prc.at[PRE_CROSS.index(r)], pair)
        else:
            pre_send(r)

    def pre_view(r):
        return p.at[r, pl.ds(zl, 1)] if r in PRE_CROSS else p.at[r]

    def pre_room(buffer, r, side):
        return buffer.at[r, side, pl.ds(0, 1)] if r in PRE_CROSS else buffer.at[r, side]

    def pre_send(r):
        mine = pre_view(r)
        copy("pa", 2 * r, mine.at[:, rows(y2, 0)], pre_room(pa, r, 0), at_y(3))
        copy("pa", 2 * r + 1, mine.at[:, rows(y2, 1)], pre_room(pa, r, 1), at_y(1))
        copy("pb", 2 * r, mine.at[:, rows(y3, 1)], pre_room(pb, r, 0), at_y(3))
        copy("pb", 2 * r + 1, mine.at[:, rows(y1, 0)], pre_room(pb, r, 1), at_y(1))

    def pre_cross(r):
        arrived("pz", r)

        @pl.loop(0, 4)
        def _(t):
            some = pl.ds(pl.multiple_of(t * 32, 32), 32)
            p[r, zl, some] = (p[r, zl, some].astype(F32) + prc[PRE_CROSS.index(r), some].astype(F32)).astype(BF16)

        pre_send(r)

    def pre_forward(r):
        mine = pre_view(r)
        for side, (block, half, device) in enumerate(((y3, 0, at_y(3)), (y1, 1, at_y(1)))):
            arrived("pa", 2 * r + side)
            spot = rows(block, half)
            mine[:, spot] = (mine[:, spot].astype(F32) + pre_room(pa, r, side)[...].astype(F32)).astype(BF16)
            copy("pc", 2 * r + side, mine.at[:, spot], pre_room(pc, r, side), device)

    def pre_block(r, hidden):
        k = 0 if r in PRE_CROSS else hidden
        low = p[r, hidden, rows(y, 0)].astype(F32) + pb[r, 1, k].astype(F32) + pc[r, 0, k].astype(F32)
        high = p[r, hidden, rows(y, 1)].astype(F32) + pb[r, 0, k].astype(F32) + pc[r, 1, k].astype(F32)
        return jnp.concatenate([low, high], axis=0)

    def pre_sum(r):
        for side in range(2):
            arrived("pb", 2 * r + side)
            arrived("pc", 2 * r + side)
        if r not in PRE_CROSS:
            ps[r] = pre_block(r, 1 - zl).astype(BF16)
            copy("pz", r, ps.at[r], pr.at[r], pair)

    def act_send(r):
        own = act.at[r, y]
        copy("as", 2 * r, own, own, at_y(3))
        copy("as", 2 * r + 1, own, own, at_y(1))

    def gelu(r):
        pre = pre_block(r, zl)
        if r not in PRE_CROSS:
            arrived("pz", r)
            pre += pr[r].astype(F32)
        value, slope[r] = gelu_parts(pre)
        act[r, y] = value.astype(BF16)

    def act_forward(r):
        arrived("as", 2 * r)
        low = act.at[r, y1, pl.ds(0, 16)]
        copy("af", 2 * r, low, low, at_y(3))
        arrived("as", 2 * r + 1)
        high = act.at[r, y3, pl.ds(16, 16)]
        copy("af", 2 * r + 1, high, high, at_y(1))

    def grad_product(r):
        lhs = cotg[r].reshape(128, 1536)
        for half in range(2):
            cols = pl.ds(half * 768, 768)
            g[r, :, cols] = jnp.dot(lhs, wt[half], preferred_element_type=F32).astype(BF16)

        copy("ga", 2 * r, g.at[r, rows(y2, 0)], ga.at[r, 0], at_y(3))
        copy("ga", 2 * r + 1, g.at[r, rows(y2, 1)], ga.at[r, 1], at_y(1))
        copy("gb", 2 * r, g.at[r, rows(y3, 1)], gb.at[r, 0], at_y(3))
        copy("gb", 2 * r + 1, g.at[r, rows(y1, 0)], gb.at[r, 1], at_y(1))

    def grad_forward(r):
        for side, (block, half, device) in enumerate(((y3, 0, at_y(3)), (y1, 1, at_y(1)))):
            arrived("ga", 2 * r + side)
            spot = rows(block, half)
            g[r, spot] = (g[r, spot].astype(F32) + ga[r, side].astype(F32)).astype(BF16)
            copy("gc", 2 * r + side, g.at[r, spot], gc.at[r, side], device)

    def hid_send(r, hidden, which):
        own = gh.at[r, hidden, y]
        copy("hs", 4 * r + 2 * which, own, own, at_y(3))
        copy("hs", 4 * r + 2 * which + 1, own, own, at_y(1))

    def hidden_grad(r):
        for side in range(2):
            arrived("gb", 2 * r + side)
            arrived("gc", 2 * r + side)
        low = g[r, rows(y, 0)].astype(F32) + gb[r, 1].astype(F32) + gc[r, 0].astype(F32)
        high = g[r, rows(y, 1)].astype(F32) + gb[r, 0].astype(F32) + gc[r, 1].astype(F32)
        gh[r, zl, y] = (jnp.concatenate([low, high], axis=0) * slope[r]).astype(BF16)
        own = gh.at[r, zl, y]
        hid_pair_send(r, 0, own)
        hid_send(r, zl, 0)

    def hid_pair_send(r, k, part):
        copy("hz", 5 * r + k, part, part, pair)

    def hidden_pair(r):
        arrived("hz", 5 * r)
        hid_send(r, 1 - zl, 1)

    def hid_rest(r):
        arrived("hf", 4 * r)
        hid_pair_send(r, 3, gh.at[r, zl, y2, pl.ds(0, 16)])
        arrived("hf", 4 * r + 1)
        hid_pair_send(r, 4, gh.at[r, zl, y2, pl.ds(16, 16)])

    def hid_forward(r, which):
        hidden = zl if which == 0 else 1 - zl
        k = 4 * r + 2 * which
        arrived("hs", k)
        low = gh.at[r, hidden, y1, pl.ds(0, 16)]
        copy("hf", k, low, low, at_y(3))
        arrived("hs", k + 1)
        high = gh.at[r, hidden, y3, pl.ds(16, 16)]
        copy("hf", k + 1, high, high, at_y(1))
        if r in HID_CROSS:
            hid_pair_send(r, 1, gh.at[r, hidden, y1])
            hid_pair_send(r, 2, gh.at[r, hidden, y3])

    def out_product(r):
        arrived("af", 2 * r)
        arrived("af", 2 * r + 1)
        for name in ("ga", "gb", "gc"):
            for side in range(2):
                left(name, 2 * r + side)
        lhs = act[r].reshape(128, 1536)
        g[r] = jnp.dot(lhs, w2[...], preferred_element_type=F32).astype(BF16)
        if r:
            copy("ox", r - 1, g.at[r], orx.at[r - 1], at_x(OFFSET[r]))

    def out_sum():
        for r in range(1, 4):
            arrived("ox", r - 1)
        total = g[0].astype(F32) + orx[0].astype(F32) + orx[1].astype(F32) + orx[2].astype(F32)
        osum[...] = total.astype(BF16).reshape(4, 32, 1536)
        for d in range(1, 4):
            copy("oz", d - 1, osum.at[lax.rem(z + d, 4)], orz.at[d - 1], at_z(d))

    def out_final():
        for d in range(1, 4):
            arrived("oz", d - 1)
        total = osum[z].astype(F32) + orz[0].astype(F32) + orz[1].astype(F32) + orz[2].astype(F32)
        out_ref[...] = total.astype(BF16)

    def second_part(whose):
        core_rows = pl.ds(pl.multiple_of((c if whose else 1 - c) * 768, 256), 768)
        lhs = actt[core_rows]
        for t in range(3):
            cols = pl.ds(t * 512, 512)
            rhs = cotg[:, :, :, cols].reshape(512, 512)
            total = jnp.dot(lhs, rhs, preferred_element_type=F32)
            if whose:
                sg_ref[:, cols] = (total + sgr[:, :, cols].reshape(768, 512).astype(F32)).astype(BF16)
            else:
                for part in range(2):
                    gone[part, :, cols] = total[part * 384 : part * 384 + 384].astype(BF16)

    def second_grad():
        for r in range(4):
            actt[:, pl.ds(r * 128, 128)] = act[r].reshape(128, 1536).T
        second_part(0)
        copy("sg", 0, gone, sgr, core)

    def second_grad_own():
        arrived("sg", 0)
        second_part(1)
        left("sg", 0)

    def in_product(r):
        if r in HID_CROSS:
            for k in range(5):
                arrived("hz", 5 * r + k)
        else:
            for k in range(4):
                arrived("hf", 4 * r + k)
        first = gh[r, 0].reshape(128, 1536)
        second = gh[r, 1].reshape(128, 1536)
        total = jnp.dot(first, wt[0], preferred_element_type=F32)
        total += jnp.dot(second, wt[1], preferred_element_type=F32)
        ig[r] = total.astype(BF16)
        if r:
            copy("ix", r - 1, ig.at[r], irx.at[r - 1], at_x(OFFSET[r]))

    def in_sum():
        for r in range(1, 4):
            arrived("ix", r - 1)
        total = ig[0].astype(F32) + irx[0].astype(F32) + irx[1].astype(F32) + irx[2].astype(F32)
        isum[...] = total.astype(BF16).reshape(4, 32, 768)
        for d in range(1, 4):
            copy("iz", d - 1, isum.at[lax.rem(z + d, 4)], irz.at[d - 1], at_z(d))

    def in_final():
        for d in range(1, 4):
            arrived("iz", d - 1)
        ig_ref[:, own_half] = (isum[z].astype(F32) + irz[1].astype(F32)).astype(BF16)
        ig_ref[:, other_half] = (irz[0].astype(F32) + irz[2].astype(F32)).astype(BF16)

    def transpose_in():
        for r in range(4):
            xgt[:, pl.ds(r * 128, 128)] = xg[r].reshape(128, 768).T

    def transpose_first():
        @pl.loop(0, 6)
        def _(t):
            cols = pl.ds(pl.multiple_of(t * 512, 512), 512)
            spot = pl.ds(pl.multiple_of(lax.rem(t, 3) * 512, 512), 512)
            wt[t // 3, spot] = w1[:, cols].T

    def transpose_second():
        @pl.loop(0, 6)
        def _(t):
            cols = pl.ds(pl.multiple_of(lax.rem(t, 3) * 512, 512), 512)
            some = pl.ds(pl.multiple_of(t // 3 * 768, 768), 768)
            wt[t // 3, cols] = w2[some, cols].T

    def first_grad(half, whose, early):
        core_rows = pl.ds(pl.multiple_of((c if whose else 1 - c) * 384, 128), 384)
        lhs = xgt[core_rows, pl.ds(256 if early else 0, 256)]
        slots = pl.ds(2 if early else 0, 2)
        if whose and not early:
            arrived("fg", half)

        wide = pl.ds(half * 1536, 1536)
        some = gh[slots, half].reshape(256, 1536)
        total = jnp.dot(lhs, some, preferred_element_type=F32)
        if whose:
            if not early:
                total += fg_ref[:, wide].astype(F32) + fgr[half].astype(F32)
            fg_ref[:, wide] = total.astype(BF16)
        else:
            if not early:
                total += gone[half].astype(F32)
            gone[half] = total.astype(BF16)

        if not whose and not early:
            copy("fg", half, gone.at[half], fgr.at[half], core)

    pre_product(0)
    pass_on("xx", "xf", xg, 1)
    pass_on("xx", "xf", xg, 0)
    load_w2.wait()
    arrived("w2", 0)
    pre_product(3)
    pre_forward(0)
    load_cot.wait()
    for k in range(3):
        arrived("cz", k)
    spread("cx", cotg)
    transpose_second()
    grad_product(0)
    arrived("xf", 0)
    arrived("xf", 1)
    pre_product(1)
    pre_forward(3)
    grad_forward(0)
    pre_product(2)
    pass_on("cx", "cf", cotg, 1)
    grad_product(3)
    pass_on("cx", "cf", cotg, 0)
    grad_product(2)
    pre_cross(1)
    grad_forward(3)
    grad_forward(2)
    transpose_in()
    arrived("cf", 0)
    arrived("cf", 1)
    pre_sum(3)
    pre_forward(1)
    grad_product(1)
    transpose_first()
    pre_cross(2)
    pre_sum(1)
    gelu(1)
    act_send(1)
    gelu(3)
    grad_forward(1)
    pre_sum(0)
    pre_forward(2)
    act_send(3)
    act_forward(1)
    hidden_grad(1)
    pre_sum(2)
    gelu(2)
    act_send(2)
    act_forward(3)
    hidden_grad(3)
    gelu(0)
    out_product(1)
    hid_forward(1, 0)
    act_forward(2)
    act_send(0)
    hidden_grad(2)
    hid_rest(1)
    hid_forward(3, 0)
    out_product(3)
    out_product(2)
    act_forward(0)
    hidden_pair(2)
    hidden_grad(0)
    hid_forward(2, 0)
    in_product(1)
    hid_rest(3)
    out_product(0)
    second_grad()
    hid_forward(2, 1)
    hidden_pair(0)
    hid_forward(0, 0)
    in_product(3)
    in_product(2)
    out_sum()
    hid_forward(0, 1)
    second_grad_own()
    for half in range(2):
        first_grad(half, 0, True)
    in_product(0)
    for half in range(2):
        first_grad(half, 0, False)
    in_sum()
    out_final()
    for half in range(2):
        first_grad(half, 1, True)
    for half in range(2):
        first_grad(half, 1, False)
    in_final()
    for made in sent.values():
        made.wait_send()


def leave(*refs):
    sems = refs[-1]
    copies = [pltpu.make_async_copy(refs[i], refs[4 + i], sems.at[i]) for i in range(4)]
    for made in copies:
        made.start()
    for made in copies:
        made.wait()


def shards(inputs, first_weight, second_weight, cotangent):
    def vmem(*shape, dtype=BF16):
        return pltpu.VMEM(shape, dtype)

    anywhere = pl.BlockSpec(memory_space=pl.ANY)
    inside = pl.BlockSpec(memory_space=pltpu.VMEM)
    shapes = [(32, 1536), (32, 1536), (384, 3072), (768, 1536)]
    results = pl.pallas_call(
        kernel,
        out_shape=[pltpu.VMEM(shape, BF16) for shape in shapes],
        in_specs=[anywhere] * 4,
        out_specs=[inside] * 4,
        scratch_shapes=[
            vmem(768, 3072), vmem(1536, 1536), vmem(2, 1536, 768), vmem(4, 4, 32, 768), vmem(768, 512), vmem(4, 4, 32, 1536),
            vmem(4, 2, 128, 1536), vmem(4, 2, 2, 16, 1536), vmem(4, 2, 2, 16, 1536), vmem(4, 2, 2, 16, 1536),
            vmem(4, 32, 1536), vmem(4, 32, 1536), vmem(len(PRE_CROSS), 128, 1536),
            vmem(4, 128, 1536), vmem(4, 2, 16, 1536), vmem(4, 2, 16, 1536), vmem(4, 2, 16, 1536),
            vmem(4, 32, 1536, dtype=F32), vmem(4, 4, 32, 1536), vmem(1536, 512), vmem(4, 2, 4, 32, 1536),
            vmem(3, 128, 1536), vmem(4, 32, 1536), vmem(3, 32, 1536),
            vmem(4, 128, 768), vmem(3, 128, 768), vmem(4, 32, 768), vmem(3, 32, 768),
            vmem(2, 384, 1536), vmem(2, 384, 1536), vmem(2, 384, 1536),
            pltpu.SemaphoreType.DMA((N_MESSAGES,)),
            pltpu.SemaphoreType.DMA((N_MESSAGES,)),
            pltpu.SemaphoreType.DMA((4,)),
        ],
        compiler_params=pltpu.CompilerParams(
            collective_id=0, has_side_effects=True, vmem_limit_bytes=50 << 20
        ),
        name="layer",
    )(inputs, first_weight, second_weight, cotangent)
    results = [pltpu.with_memory_space_constraint(result, pltpu.VMEM) for result in results]
    return pl.pallas_call(
        leave,
        out_shape=[jax.ShapeDtypeStruct(shape, BF16) for shape in shapes],
        in_specs=[inside] * 4,
        out_specs=[anywhere] * 4,
        scratch_shapes=[pltpu.SemaphoreType.DMA((4,))],
        compiler_params=pltpu.CompilerParams(vmem_limit_bytes=1 << 20),
        name="leave",
    )(*results)


def solution(mesh):
    in_specs = (
        P(("ia", "al"), "ja"),
        P(("ja", "ia"), "al"),
        P(("al", "ia"), "ja"),
        P(("ia", "al"), "ja"),
    )
    out_specs = (
        P(("ia", "al"), "ja"),
        P(("ia", "al"), "ja"),
        P(("ja", "ia"), "al"),
        P(("al", "ia"), "ja"),
    )
    return jax.shard_map(shards, mesh=mesh, in_specs=in_specs, out_specs=out_specs, check_vma=False)
```

```python
import jax
import jax.numpy as jnp
from jax import lax
from jax.experimental import pallas as pl
from jax.experimental.pallas import tpu as pltpu
from jax.sharding import PartitionSpec as P

BF16, F32 = jnp.bfloat16, jnp.float32
MESH = pl.DeviceIdType.MESH

OFFSET = (0, 2, 1, 3)
SLOT = {offset: slot for slot, offset in enumerate(OFFSET)}
PRE_CROSS = (2, 1)
HID_CROSS = (1, 2, 3)


def gelu_parts(pre):
    scaled = pre * 0.7071067811865476
    cdf = 0.5 * (1.0 + lax.erf(scaled))
    value = pre * cdf
    slope = cdf + pre * jnp.exp(-0.5 * pre * pre) * 0.3989422804014327
    return (value, slope)


MESSAGES = {}


def number(name, count):
    MESSAGES[name] = sum(size for _, size in LAYOUT[:[n for n, _ in LAYOUT].index(name)])
    return count


LAYOUT = [
    ("xz", 3), ("xx", 8), ("xf", 2), ("cz", 3), ("cx", 2), ("cf", 2), ("w1", 1), ("w2", 1),
    ("pa", 8), ("pb", 8), ("pc", 8), ("pz", 4),
    ("ga", 8), ("gb", 8), ("gc", 8),
    ("as", 8), ("af", 8), ("hz", 20), ("hs", 16), ("hf", 16),
    ("ox", 3), ("oz", 3), ("ix", 3), ("iz", 3), ("sg", 1), ("fg", 2),
]
for _name, _count in LAYOUT:
    number(_name, _count)
N_MESSAGES = sum(size for _, size in LAYOUT)


def kernel(
    x_ref, w1_ref, w2_ref, cot_ref,
    out_ref, ig_ref, fg_ref, sg_ref,
    w1, w2, wt, xg, xgt, cotg,
    p, pa, pb, pc, ps, pr, prc,
    g, ga, gb, gc,
    slope, act, actt, gh,
    orx, osum, orz,
    ig, irx, isum, irz,
    gone, sgr, fgr,
    send_sem, recv_sem, local_sem,
):
    ia, y, al = lax.axis_index("ia"), lax.axis_index("ja"), lax.axis_index("al")
    x, z, zl, c = al // 2, lax.rem(al, 2) * 2 + ia // 2, ia // 2, lax.rem(ia, 2)

    def at_x(d):
        return (ia, y, lax.rem(x + d + 4, 4) * 2 + lax.rem(al, 2))

    def at_y(d):
        return (ia, lax.rem(y + d + 4, 4), al)

    def at_z(d):
        other = lax.rem(z + d + 4, 4)
        return (lax.rem(other, 2) * 2 + c, y, x * 2 + other // 2)

    core = (zl * 2 + 1 - c, y, al)
    pair = ((1 - zl) * 2 + c, y, al)
    y1, y2, y3 = lax.rem(y + 1, 4), lax.rem(y + 2, 4), lax.rem(y + 3, 4)

    barrier = pltpu.get_barrier_semaphore()
    partners = [at_x(1), at_x(2), at_x(3), at_y(1), at_y(3), at_z(1), at_z(2), at_z(3), core]
    for partner in partners:
        pl.semaphore_signal(barrier, inc=1, device_id=partner, device_id_type=MESH)

    sent = {}

    def copy(name, k, src, dst, device):
        i = MESSAGES[name] + k
        made = pltpu.make_async_remote_copy(
            src_ref=src, dst_ref=dst, send_sem=send_sem.at[i], recv_sem=recv_sem.at[i],
            device_id=device, device_id_type=MESH,
        )
        made.start()
        sent[(name, k)] = made

    def left(name, k):
        sent.pop((name, k)).wait_send()

    def arrived(name, k):
        sent[(name, k)].wait_recv()

    n_local = [0]

    def local(src, dst):
        made = pltpu.make_async_copy(src, dst, local_sem.at[n_local[0]])
        made.start()
        n_local[0] += 1
        return made

    own_half = pl.ds(pl.multiple_of(zl * 768, 768), 768)
    other_half = pl.ds(pl.multiple_of((1 - zl) * 768, 768), 768)
    w1_rows = pl.ds(pl.multiple_of(c * 384, 384), 384)
    w2_rows = pl.ds(pl.multiple_of(c * 768, 768), 768)
    load_x = local(x_ref.at[:, own_half], xg.at[0, z])
    load_w1 = local(w1_ref, w1.at[w1_rows])
    load_cot = local(cot_ref, cotg.at[0, z])
    load_w2 = local(w2_ref, w2.at[w2_rows])

    pl.semaphore_wait(barrier, len(partners))

    copy("xz", 0, x_ref.at[:, other_half], xg.at[0, z], at_z(1))
    copy("xz", 2, x_ref.at[:, other_half], xg.at[0, z], at_z(3))
    copy("xz", 1, x_ref.at[:, own_half], xg.at[0, z], at_z(2))
    copy("w1", 0, w1_ref, w1.at[w1_rows], core)
    for d in (1, 3, 2):
        copy("cz", d - 1, cot_ref, cotg.at[0, z], at_z(d))
    copy("w2", 0, w2_ref, w2.at[w2_rows], core)

    def spread(name, buffer):
        copy(name, 0, buffer.at[0], buffer.at[SLOT[1]], at_x(3))
        copy(name, 1, buffer.at[0], buffer.at[SLOT[3]], at_x(1))

    def spread_block(k, block):
        copy("xx", k, xg.at[0, block], xg.at[SLOT[1], block], at_x(3))
        copy("xx", 4 + k, xg.at[0, block], xg.at[SLOT[3], block], at_x(1))

    def pass_on(name, far, buffer, side):
        for k in range(4 * side, 4 * side + 4) if name == "xx" else (side,):
            arrived(name, k)
        slot, half, device = ((SLOT[1], 0, at_x(3)), (SLOT[3], 2, at_x(1)))[side]
        part = pl.ds(half, 2)
        copy(far, side, buffer.at[slot, part], buffer.at[SLOT[2], part], device)

    load_x.wait()
    spread_block(0, z)
    for k, (message, step) in enumerate(((0, 3), (2, 1), (1, 2))):
        arrived("xz", message)
        spread_block(k + 1, lax.rem(z + step, 4))
    load_w1.wait()
    arrived("w1", 0)

    def rows(block, half):
        return pl.ds(pl.multiple_of(block * 32 + half * 16, 16), 16)

    def pre_product(r):
        lhs = xg[r].reshape(128, 768)

        for half in range(2):
            cols = pl.ds(half * 1536, 1536)
            p[r, half] = jnp.dot(lhs, w1[:, cols], preferred_element_type=F32).astype(BF16)

        if r in PRE_CROSS:
            copy("pz", r, p.at[r, 1 - zl], prc.at[PRE_CROSS.index(r)], pair)
        else:
            pre_send(r)

    def pre_view(r):
        return p.at[r, pl.ds(zl, 1)] if r in PRE_CROSS else p.at[r]

    def pre_room(buffer, r, side):
        return buffer.at[r, side, pl.ds(0, 1)] if r in PRE_CROSS else buffer.at[r, side]

    def pre_send(r):
        mine = pre_view(r)
        copy("pa", 2 * r, mine.at[:, rows(y2, 0)], pre_room(pa, r, 0), at_y(3))
        copy("pa", 2 * r + 1, mine.at[:, rows(y2, 1)], pre_room(pa, r, 1), at_y(1))
        copy("pb", 2 * r, mine.at[:, rows(y3, 1)], pre_room(pb, r, 0), at_y(3))
        copy("pb", 2 * r + 1, mine.at[:, rows(y1, 0)], pre_room(pb, r, 1), at_y(1))

    def pre_cross(r):
        arrived("pz", r)

        @pl.loop(0, 4)
        def _(t):
            some = pl.ds(pl.multiple_of(t * 32, 32), 32)
            p[r, zl, some] = (p[r, zl, some].astype(F32) + prc[PRE_CROSS.index(r), some].astype(F32)).astype(BF16)

        pre_send(r)

    def pre_forward(r):
        mine = pre_view(r)
        for side, (block, half, device) in enumerate(((y3, 0, at_y(3)), (y1, 1, at_y(1)))):
            arrived("pa", 2 * r + side)
            spot = rows(block, half)
            mine[:, spot] = (mine[:, spot].astype(F32) + pre_room(pa, r, side)[...].astype(F32)).astype(BF16)
            copy("pc", 2 * r + side, mine.at[:, spot], pre_room(pc, r, side), device)

    def pre_block(r, hidden):
        k = 0 if r in PRE_CROSS else hidden
        low = p[r, hidden, rows(y, 0)].astype(F32) + pb[r, 1, k].astype(F32) + pc[r, 0, k].astype(F32)
        high = p[r, hidden, rows(y, 1)].astype(F32) + pb[r, 0, k].astype(F32) + pc[r, 1, k].astype(F32)
        return jnp.concatenate([low, high], axis=0)

    def pre_sum(r):
        for side in range(2):
            arrived("pb", 2 * r + side)
            arrived("pc", 2 * r + side)
        if r not in PRE_CROSS:
            ps[r] = pre_block(r, 1 - zl).astype(BF16)
            copy("pz", r, ps.at[r], pr.at[r], pair)

    def act_send(r):
        own = act.at[r, y]
        copy("as", 2 * r, own, own, at_y(3))
        copy("as", 2 * r + 1, own, own, at_y(1))

    def gelu(r):
        pre = pre_block(r, zl)
        if r not in PRE_CROSS:
            arrived("pz", r)
            pre += pr[r].astype(F32)
        value, slope[r] = gelu_parts(pre)
        act[r, y] = value.astype(BF16)

    def act_forward(r):
        arrived("as", 2 * r)
        low = act.at[r, y1, pl.ds(0, 16)]
        copy("af", 2 * r, low, low, at_y(3))
        arrived("as", 2 * r + 1)
        high = act.at[r, y3, pl.ds(16, 16)]
        copy("af", 2 * r + 1, high, high, at_y(1))

    def grad_product(r):
        lhs = cotg[r].reshape(128, 1536)
        for half in range(2):
            cols = pl.ds(half * 768, 768)
            g[r, :, cols] = jnp.dot(lhs, wt[half], preferred_element_type=F32).astype(BF16)

        copy("ga", 2 * r, g.at[r, rows(y2, 0)], ga.at[r, 0], at_y(3))
        copy("ga", 2 * r + 1, g.at[r, rows(y2, 1)], ga.at[r, 1], at_y(1))
        copy("gb", 2 * r, g.at[r, rows(y3, 1)], gb.at[r, 0], at_y(3))
        copy("gb", 2 * r + 1, g.at[r, rows(y1, 0)], gb.at[r, 1], at_y(1))

    def grad_forward(r):
        for side, (block, half, device) in enumerate(((y3, 0, at_y(3)), (y1, 1, at_y(1)))):
            arrived("ga", 2 * r + side)
            spot = rows(block, half)
            g[r, spot] = (g[r, spot].astype(F32) + ga[r, side].astype(F32)).astype(BF16)
            copy("gc", 2 * r + side, g.at[r, spot], gc.at[r, side], device)

    def hid_send(r, hidden, which):
        own = gh.at[r, hidden, y]
        copy("hs", 4 * r + 2 * which, own, own, at_y(3))
        copy("hs", 4 * r + 2 * which + 1, own, own, at_y(1))

    def hidden_grad(r):
        for side in range(2):
            arrived("gb", 2 * r + side)
            arrived("gc", 2 * r + side)
        low = g[r, rows(y, 0)].astype(F32) + gb[r, 1].astype(F32) + gc[r, 0].astype(F32)
        high = g[r, rows(y, 1)].astype(F32) + gb[r, 0].astype(F32) + gc[r, 1].astype(F32)
        gh[r, zl, y] = (jnp.concatenate([low, high], axis=0) * slope[r]).astype(BF16)
        own = gh.at[r, zl, y]
        hid_pair_send(r, 0, own)
        hid_send(r, zl, 0)

    def hid_pair_send(r, k, part):
        copy("hz", 5 * r + k, part, part, pair)

    def hidden_pair(r):
        arrived("hz", 5 * r)
        hid_send(r, 1 - zl, 1)

    def hid_rest(r):
        arrived("hf", 4 * r)
        hid_pair_send(r, 3, gh.at[r, zl, y2, pl.ds(0, 16)])
        arrived("hf", 4 * r + 1)
        hid_pair_send(r, 4, gh.at[r, zl, y2, pl.ds(16, 16)])

    def hid_forward(r, which):
        hidden = zl if which == 0 else 1 - zl
        k = 4 * r + 2 * which
        arrived("hs", k)
        low = gh.at[r, hidden, y1, pl.ds(0, 16)]
        copy("hf", k, low, low, at_y(3))
        arrived("hs", k + 1)
        high = gh.at[r, hidden, y3, pl.ds(16, 16)]
        copy("hf", k + 1, high, high, at_y(1))
        if r in HID_CROSS:
            hid_pair_send(r, 1, gh.at[r, hidden, y1])
            hid_pair_send(r, 2, gh.at[r, hidden, y3])

    def out_product(r):
        arrived("af", 2 * r)
        arrived("af", 2 * r + 1)
        for name in ("ga", "gb", "gc"):
            for side in range(2):
                left(name, 2 * r + side)
        lhs = act[r].reshape(128, 1536)
        g[r] = jnp.dot(lhs, w2[...], preferred_element_type=F32).astype(BF16)
        if r:
            copy("ox", r - 1, g.at[r], orx.at[r - 1], at_x(OFFSET[r]))

    def out_sum():
        for r in range(1, 4):
            arrived("ox", r - 1)
        total = g[0].astype(F32) + orx[0].astype(F32) + orx[1].astype(F32) + orx[2].astype(F32)
        osum[...] = total.astype(BF16).reshape(4, 32, 1536)
        for d in range(1, 4):
            copy("oz", d - 1, osum.at[lax.rem(z + d, 4)], orz.at[d - 1], at_z(d))

    def out_final():
        for d in range(1, 4):
            arrived("oz", d - 1)
        total = osum[z].astype(F32) + orz[0].astype(F32) + orz[1].astype(F32) + orz[2].astype(F32)
        out_ref[...] = total.astype(BF16)

    def second_part(whose):
        core_rows = pl.ds(pl.multiple_of((c if whose else 1 - c) * 768, 256), 768)
        lhs = actt[core_rows]
        for t in range(3):
            cols = pl.ds(t * 512, 512)
            rhs = cotg[:, :, :, cols].reshape(512, 512)
            total = jnp.dot(lhs, rhs, preferred_element_type=F32)
            if whose:
                sg_ref[:, cols] = (total + sgr[:, :, cols].reshape(768, 512).astype(F32)).astype(BF16)
            else:
                for part in range(2):
                    gone[part, :, cols] = total[part * 384 : part * 384 + 384].astype(BF16)

    def second_grad():
        for r in range(4):
            actt[:, pl.ds(r * 128, 128)] = act[r].reshape(128, 1536).T
        second_part(0)
        copy("sg", 0, gone, sgr, core)

    def second_grad_own():
        arrived("sg", 0)
        second_part(1)
        left("sg", 0)

    def in_product(r):
        if r in HID_CROSS:
            for k in range(5):
                arrived("hz", 5 * r + k)
        else:
            for k in range(4):
                arrived("hf", 4 * r + k)
        first = gh[r, 0].reshape(128, 1536)
        second = gh[r, 1].reshape(128, 1536)
        total = jnp.dot(first, wt[0], preferred_element_type=F32)
        total += jnp.dot(second, wt[1], preferred_element_type=F32)
        ig[r] = total.astype(BF16)
        if r:
            copy("ix", r - 1, ig.at[r], irx.at[r - 1], at_x(OFFSET[r]))

    def in_sum():
        for r in range(1, 4):
            arrived("ix", r - 1)
        total = ig[0].astype(F32) + irx[0].astype(F32) + irx[1].astype(F32) + irx[2].astype(F32)
        isum[...] = total.astype(BF16).reshape(4, 32, 768)
        for d in range(1, 4):
            copy("iz", d - 1, isum.at[lax.rem(z + d, 4)], irz.at[d - 1], at_z(d))

    def in_final():
        for d in range(1, 4):
            arrived("iz", d - 1)
        ig_ref[:, own_half] = (isum[z].astype(F32) + irz[1].astype(F32)).astype(BF16)
        ig_ref[:, other_half] = (irz[0].astype(F32) + irz[2].astype(F32)).astype(BF16)

    def transpose_in():
        for r in range(4):
            xgt[:, pl.ds(r * 128, 128)] = xg[r].reshape(128, 768).T

    def transpose_first():
        @pl.loop(0, 6)
        def _(t):
            cols = pl.ds(pl.multiple_of(t * 512, 512), 512)
            spot = pl.ds(pl.multiple_of(lax.rem(t, 3) * 512, 512), 512)
            wt[t // 3, spot] = w1[:, cols].T

    def transpose_second():
        @pl.loop(0, 6)
        def _(t):
            cols = pl.ds(pl.multiple_of(lax.rem(t, 3) * 512, 512), 512)
            some = pl.ds(pl.multiple_of(t // 3 * 768, 768), 768)
            wt[t // 3, cols] = w2[some, cols].T

    def first_grad(half, whose, early):
        core_rows = pl.ds(pl.multiple_of((c if whose else 1 - c) * 384, 128), 384)
        depth = 384 if early else 128
        lhs = xgt[core_rows, pl.ds(128 if early else 0, depth)]
        slots = pl.ds(1, 3) if early else pl.ds(0, 1)
        if whose and not early:
            arrived("fg", half)

        wide = pl.ds(half * 1536, 1536)
        some = gh[slots, half].reshape(depth, 1536)
        total = jnp.dot(lhs, some, preferred_element_type=F32)
        if whose:
            if not early:
                total += fg_ref[:, wide].astype(F32) + fgr[half].astype(F32)
            fg_ref[:, wide] = total.astype(BF16)
        else:
            if not early:
                total += gone[half].astype(F32)
            gone[half] = total.astype(BF16)

        if not whose and not early:
            copy("fg", half, gone.at[half], fgr.at[half], core)

    pre_product(0)
    pass_on("xx", "xf", xg, 0)
    pre_product(2)
    pass_on("xx", "xf", xg, 1)
    pre_product(3)
    pre_forward(0)
    load_cot.wait()
    for k in range(3):
        arrived("cz", k)
    spread("cx", cotg)
    load_w2.wait()
    arrived("w2", 0)
    transpose_second()
    arrived("xf", 0)
    arrived("xf", 1)
    grad_product(0)
    pre_product(1)
    pre_forward(3)
    pre_cross(2)
    pass_on("cx", "cf", cotg, 0)
    grad_product(2)
    pass_on("cx", "cf", cotg, 1)
    pre_forward(2)
    grad_product(3)
    grad_forward(2)
    pre_cross(1)
    pre_sum(3)
    pre_sum(0)
    arrived("cf", 0)
    arrived("cf", 1)
    pre_sum(2)
    gelu(2)
    grad_product(1)
    pre_forward(1)
    gelu(3)
    hidden_grad(2)
    transpose_first()
    grad_forward(1)
    pre_sum(1)
    gelu(1)
    act_send(1)
    act_send(3)
    hid_forward(2, 0)
    act_forward(1)
    hidden_grad(1)
    act_send(2)
    gelu(0)
    hid_rest(2)
    out_product(1)
    grad_forward(3)
    hid_forward(1, 0)
    act_forward(2)
    act_forward(3)
    grad_forward(0)
    hid_rest(1)
    hidden_grad(3)
    act_send(0)
    out_product(2)
    out_product(3)
    hidden_grad(0)
    hid_forward(3, 0)
    in_product(1)
    act_forward(0)
    in_product(2)
    hidden_pair(0)
    hid_rest(3)
    hid_forward(0, 0)
    transpose_in()
    out_product(0)
    second_grad()
    hid_forward(0, 1)
    in_product(3)
    out_sum()
    in_product(0)
    second_grad_own()
    for half in range(2):
        first_grad(half, 0, True)
    in_sum()
    for half in range(2):
        first_grad(half, 0, False)
    for half in range(2):
        first_grad(half, 1, True)
    out_final()
    for half in range(2):
        first_grad(half, 1, False)
    in_final()
    for made in sent.values():
        made.wait_send()


def leave(*refs):
    sems = refs[-1]
    copies = [pltpu.make_async_copy(refs[i], refs[4 + i], sems.at[i]) for i in range(4)]
    for made in copies:
        made.start()
    for made in copies:
        made.wait()


def shards(inputs, first_weight, second_weight, cotangent):
    def vmem(*shape, dtype=BF16):
        return pltpu.VMEM(shape, dtype)

    anywhere = pl.BlockSpec(memory_space=pl.ANY)
    inside = pl.BlockSpec(memory_space=pltpu.VMEM)
    shapes = [(32, 1536), (32, 1536), (384, 3072), (768, 1536)]
    results = pl.pallas_call(
        kernel,
        out_shape=[pltpu.VMEM(shape, BF16) for shape in shapes],
        in_specs=[anywhere] * 4,
        out_specs=[inside] * 4,
        scratch_shapes=[
            vmem(768, 3072), vmem(1536, 1536), vmem(2, 1536, 768), vmem(4, 4, 32, 768), vmem(768, 512), vmem(4, 4, 32, 1536),
            vmem(4, 2, 128, 1536), vmem(4, 2, 2, 16, 1536), vmem(4, 2, 2, 16, 1536), vmem(4, 2, 2, 16, 1536),
            vmem(4, 32, 1536), vmem(4, 32, 1536), vmem(len(PRE_CROSS), 128, 1536),
            vmem(4, 128, 1536), vmem(4, 2, 16, 1536), vmem(4, 2, 16, 1536), vmem(4, 2, 16, 1536),
            vmem(4, 32, 1536, dtype=F32), vmem(4, 4, 32, 1536), vmem(1536, 512), vmem(4, 2, 4, 32, 1536),
            vmem(3, 128, 1536), vmem(4, 32, 1536), vmem(3, 32, 1536),
            vmem(4, 128, 768), vmem(3, 128, 768), vmem(4, 32, 768), vmem(3, 32, 768),
            vmem(2, 384, 1536), vmem(2, 384, 1536), vmem(2, 384, 1536),
            pltpu.SemaphoreType.DMA((N_MESSAGES,)),
            pltpu.SemaphoreType.DMA((N_MESSAGES,)),
            pltpu.SemaphoreType.DMA((4,)),
        ],
        compiler_params=pltpu.CompilerParams(
            collective_id=0, has_side_effects=True, vmem_limit_bytes=50 << 20
        ),
        name="layer",
    )(inputs, first_weight, second_weight, cotangent)
    results = [pltpu.with_memory_space_constraint(result, pltpu.VMEM) for result in results]
    return pl.pallas_call(
        leave,
        out_shape=[jax.ShapeDtypeStruct(shape, BF16) for shape in shapes],
        in_specs=[inside] * 4,
        out_specs=[anywhere] * 4,
        scratch_shapes=[pltpu.SemaphoreType.DMA((4,))],
        compiler_params=pltpu.CompilerParams(vmem_limit_bytes=1 << 20),
        name="leave",
    )(*results)


def solution(mesh):
    in_specs = (
        P(("ia", "al"), "ja"),
        P(("ja", "ia"), "al"),
        P(("al", "ia"), "ja"),
        P(("ia", "al"), "ja"),
    )
    out_specs = (
        P(("ia", "al"), "ja"),
        P(("ia", "al"), "ja"),
        P(("ja", "ia"), "al"),
        P(("al", "ia"), "ja"),
    )
    return jax.shard_map(shards, mesh=mesh, in_specs=in_specs, out_specs=out_specs, check_vma=False)
```

```python
import jax
import jax.numpy as jnp
from jax import lax
from jax.experimental import pallas as pl
from jax.experimental.pallas import tpu as pltpu
from jax.sharding import PartitionSpec as P

BF16, F32 = jnp.bfloat16, jnp.float32
MESH = pl.DeviceIdType.MESH

OFFSET = (0, 2, 1, 3)
SLOT = {offset: slot for slot, offset in enumerate(OFFSET)}
PRE_CROSS = (2, 1)
HID_CROSS = (1, 2, 3)


def gelu_parts(pre):
    scaled = pre * 0.7071067811865476
    cdf = 0.5 * (1.0 + lax.erf(scaled))
    value = pre * cdf
    slope = cdf + pre * jnp.exp(-0.5 * pre * pre) * 0.3989422804014327
    return (value, slope)


MESSAGES = {}


def number(name, count):
    MESSAGES[name] = sum(size for _, size in LAYOUT[:[n for n, _ in LAYOUT].index(name)])
    return count


LAYOUT = [
    ("xz", 3), ("xx", 8), ("xf", 2), ("cz", 3), ("cx", 2), ("cf", 2), ("w1", 1), ("w2", 1),
    ("pa", 8), ("pb", 8), ("pc", 8), ("pz", 4), ("qa", 4), ("qb", 4),
    ("ga", 8), ("gb", 8), ("gc", 8),
    ("as", 8), ("af", 8), ("hz", 20), ("hs", 16), ("hf", 16),
    ("ox", 3), ("oz", 3), ("ix", 3), ("iz", 3), ("sg", 1), ("fg", 2),
]
for _name, _count in LAYOUT:
    number(_name, _count)
N_MESSAGES = sum(size for _, size in LAYOUT)


def kernel(
    x_ref, w1_ref, w2_ref, cot_ref,
    out_ref, ig_ref, fg_ref, sg_ref,
    w1, w2, wt, xg, xgt, cotg,
    p, pa, pb, pc, ps, pr, prc,
    g, ga, gb, gc,
    slope, act, actt, gh,
    orx, osum, orz,
    ig, irx, isum, irz,
    gone, sgr, fgr,
    send_sem, recv_sem, local_sem,
):
    ia, y, al = lax.axis_index("ia"), lax.axis_index("ja"), lax.axis_index("al")
    x, z, zl, c = al // 2, lax.rem(al, 2) * 2 + ia // 2, ia // 2, lax.rem(ia, 2)

    def at_x(d):
        return (ia, y, lax.rem(x + d + 4, 4) * 2 + lax.rem(al, 2))

    def at_y(d):
        return (ia, lax.rem(y + d + 4, 4), al)

    def at_z(d):
        other = lax.rem(z + d + 4, 4)
        return (lax.rem(other, 2) * 2 + c, y, x * 2 + other // 2)

    core = (zl * 2 + 1 - c, y, al)
    pair = ((1 - zl) * 2 + c, y, al)
    y1, y2, y3 = lax.rem(y + 1, 4), lax.rem(y + 2, 4), lax.rem(y + 3, 4)

    barrier = pltpu.get_barrier_semaphore()
    partners = [at_x(1), at_x(2), at_x(3), at_y(1), at_y(3), at_z(1), at_z(2), at_z(3), core]
    for partner in partners:
        pl.semaphore_signal(barrier, inc=1, device_id=partner, device_id_type=MESH)

    sent = {}

    def copy(name, k, src, dst, device):
        i = MESSAGES[name] + k
        made = pltpu.make_async_remote_copy(
            src_ref=src, dst_ref=dst, send_sem=send_sem.at[i], recv_sem=recv_sem.at[i],
            device_id=device, device_id_type=MESH,
        )
        made.start()
        sent[(name, k)] = made

    def left(name, k):
        sent.pop((name, k)).wait_send()

    def arrived(name, k):
        sent[(name, k)].wait_recv()

    n_local = [0]

    def local(src, dst):
        made = pltpu.make_async_copy(src, dst, local_sem.at[n_local[0]])
        made.start()
        n_local[0] += 1
        return made

    own_half = pl.ds(pl.multiple_of(zl * 768, 768), 768)
    other_half = pl.ds(pl.multiple_of((1 - zl) * 768, 768), 768)
    w1_rows = pl.ds(pl.multiple_of(c * 384, 384), 384)
    w2_rows = pl.ds(pl.multiple_of(c * 768, 768), 768)
    load_x = local(x_ref.at[:, own_half], xg.at[0, z])
    load_w1 = local(w1_ref, w1.at[w1_rows])
    load_cot = local(cot_ref, cotg.at[0, z])
    load_w2 = local(w2_ref, w2.at[w2_rows])

    pl.semaphore_wait(barrier, len(partners))

    copy("xz", 0, x_ref.at[:, other_half], xg.at[0, z], at_z(1))
    copy("xz", 2, x_ref.at[:, other_half], xg.at[0, z], at_z(3))
    copy("xz", 1, x_ref.at[:, own_half], xg.at[0, z], at_z(2))
    copy("w1", 0, w1_ref, w1.at[w1_rows], core)
    for d in (1, 3, 2):
        copy("cz", d - 1, cot_ref, cotg.at[0, z], at_z(d))
    copy("w2", 0, w2_ref, w2.at[w2_rows], core)

    def spread(name, buffer):
        copy(name, 0, buffer.at[0], buffer.at[SLOT[1]], at_x(3))
        copy(name, 1, buffer.at[0], buffer.at[SLOT[3]], at_x(1))

    def spread_block(k, block):
        copy("xx", k, xg.at[0, block], xg.at[SLOT[1], block], at_x(3))
        copy("xx", 4 + k, xg.at[0, block], xg.at[SLOT[3], block], at_x(1))

    def pass_on(name, far, buffer, side):
        for k in range(4 * side, 4 * side + 4) if name == "xx" else (side,):
            arrived(name, k)
        slot, half, device = ((SLOT[1], 0, at_x(3)), (SLOT[3], 2, at_x(1)))[side]
        part = pl.ds(half, 2)
        copy(far, side, buffer.at[slot, part], buffer.at[SLOT[2], part], device)

    load_x.wait()
    spread_block(0, z)
    for k, (message, step) in enumerate(((0, 3), (2, 1), (1, 2))):
        arrived("xz", message)
        spread_block(k + 1, lax.rem(z + step, 4))
    load_w1.wait()
    arrived("w1", 0)

    def rows(block, half):
        return pl.ds(pl.multiple_of(block * 32 + half * 16, 16), 16)

    def pre_product(r):
        lhs = xg[r].reshape(128, 768)

        for half in range(2):
            cols = pl.ds(half * 1536, 1536)
            p[r, half] = jnp.dot(lhs, w1[:, cols], preferred_element_type=F32).astype(BF16)
            if r == 0:
                pre_send_half(half)

        if r in PRE_CROSS:
            copy("pz", r, p.at[r, 1 - zl], prc.at[PRE_CROSS.index(r)], pair)
        elif r:
            pre_send(r)

    def pre_send_half(half):
        copy("qa", half, p.at[0, half, rows(y2, 0)], pa.at[0, 0, half], at_y(3))
        copy("qa", 2 + half, p.at[0, half, rows(y2, 1)], pa.at[0, 1, half], at_y(1))
        copy("qb", half, p.at[0, half, rows(y3, 1)], pb.at[0, 0, half], at_y(3))
        copy("qb", 2 + half, p.at[0, half, rows(y1, 0)], pb.at[0, 1, half], at_y(1))

    def pre_arrived(name, r, side):
        if r:
            arrived("p" + name, 2 * r + side)
        else:
            arrived("q" + name, 2 * side)
            arrived("q" + name, 2 * side + 1)

    def pre_view(r):
        return p.at[r, pl.ds(zl, 1)] if r in PRE_CROSS else p.at[r]

    def pre_room(buffer, r, side):
        return buffer.at[r, side, pl.ds(0, 1)] if r in PRE_CROSS else buffer.at[r, side]

    def pre_send(r):
        mine = pre_view(r)
        copy("pa", 2 * r, mine.at[:, rows(y2, 0)], pre_room(pa, r, 0), at_y(3))
        copy("pa", 2 * r + 1, mine.at[:, rows(y2, 1)], pre_room(pa, r, 1), at_y(1))
        copy("pb", 2 * r, mine.at[:, rows(y3, 1)], pre_room(pb, r, 0), at_y(3))
        copy("pb", 2 * r + 1, mine.at[:, rows(y1, 0)], pre_room(pb, r, 1), at_y(1))

    def pre_cross(r):
        arrived("pz", r)

        @pl.loop(0, 4)
        def _(t):
            some = pl.ds(pl.multiple_of(t * 32, 32), 32)
            p[r, zl, some] = (p[r, zl, some].astype(F32) + prc[PRE_CROSS.index(r), some].astype(F32)).astype(BF16)

        pre_send(r)

    def pre_forward(r):
        mine = pre_view(r)
        for side, (block, half, device) in enumerate(((y3, 0, at_y(3)), (y1, 1, at_y(1)))):
            pre_arrived("a", r, side)
            spot = rows(block, half)
            mine[:, spot] = (mine[:, spot].astype(F32) + pre_room(pa, r, side)[...].astype(F32)).astype(BF16)
            copy("pc", 2 * r + side, mine.at[:, spot], pre_room(pc, r, side), device)

    def pre_block(r, hidden):
        k = 0 if r in PRE_CROSS else hidden
        low = p[r, hidden, rows(y, 0)].astype(F32) + pb[r, 1, k].astype(F32) + pc[r, 0, k].astype(F32)
        high = p[r, hidden, rows(y, 1)].astype(F32) + pb[r, 0, k].astype(F32) + pc[r, 1, k].astype(F32)
        return jnp.concatenate([low, high], axis=0)

    def pre_sum(r):
        for side in range(2):
            pre_arrived("b", r, side)
            arrived("pc", 2 * r + side)
        if r not in PRE_CROSS:
            ps[r] = pre_block(r, 1 - zl).astype(BF16)
            copy("pz", r, ps.at[r], pr.at[r], pair)

    def act_send(r):
        own = act.at[r, y]
        copy("as", 2 * r, own, own, at_y(3))
        copy("as", 2 * r + 1, own, own, at_y(1))

    def gelu(r):
        pre = pre_block(r, zl)
        if r not in PRE_CROSS:
            arrived("pz", r)
            pre += pr[r].astype(F32)
        value, slope[r] = gelu_parts(pre)
        act[r, y] = value.astype(BF16)

    def act_forward(r):
        arrived("as", 2 * r)
        low = act.at[r, y1, pl.ds(0, 16)]
        copy("af", 2 * r, low, low, at_y(3))
        arrived("as", 2 * r + 1)
        high = act.at[r, y3, pl.ds(16, 16)]
        copy("af", 2 * r + 1, high, high, at_y(1))

    def grad_product(r):
        lhs = cotg[r].reshape(128, 1536)
        for half in range(2):
            cols = pl.ds(half * 768, 768)
            g[r, :, cols] = jnp.dot(lhs, wt[half], preferred_element_type=F32).astype(BF16)

        copy("ga", 2 * r, g.at[r, rows(y2, 0)], ga.at[r, 0], at_y(3))
        copy("ga", 2 * r + 1, g.at[r, rows(y2, 1)], ga.at[r, 1], at_y(1))
        copy("gb", 2 * r, g.at[r, rows(y3, 1)], gb.at[r, 0], at_y(3))
        copy("gb", 2 * r + 1, g.at[r, rows(y1, 0)], gb.at[r, 1], at_y(1))

    def grad_forward(r):
        for side, (block, half, device) in enumerate(((y3, 0, at_y(3)), (y1, 1, at_y(1)))):
            arrived("ga", 2 * r + side)
            spot = rows(block, half)
            g[r, spot] = (g[r, spot].astype(F32) + ga[r, side].astype(F32)).astype(BF16)
            copy("gc", 2 * r + side, g.at[r, spot], gc.at[r, side], device)

    def hid_send(r, hidden, which):
        own = gh.at[r, hidden, y]
        copy("hs", 4 * r + 2 * which, own, own, at_y(3))
        copy("hs", 4 * r + 2 * which + 1, own, own, at_y(1))

    def hidden_grad(r):
        for side in range(2):
            arrived("gb", 2 * r + side)
            arrived("gc", 2 * r + side)
        low = g[r, rows(y, 0)].astype(F32) + gb[r, 1].astype(F32) + gc[r, 0].astype(F32)
        high = g[r, rows(y, 1)].astype(F32) + gb[r, 0].astype(F32) + gc[r, 1].astype(F32)
        gh[r, zl, y] = (jnp.concatenate([low, high], axis=0) * slope[r]).astype(BF16)
        own = gh.at[r, zl, y]
        hid_pair_send(r, 0, own)
        hid_send(r, zl, 0)

    def hid_pair_send(r, k, part):
        copy("hz", 5 * r + k, part, part, pair)

    def hidden_pair(r):
        arrived("hz", 5 * r)
        hid_send(r, 1 - zl, 1)

    def hid_rest(r):
        arrived("hf", 4 * r)
        hid_pair_send(r, 3, gh.at[r, zl, y2, pl.ds(0, 16)])
        arrived("hf", 4 * r + 1)
        hid_pair_send(r, 4, gh.at[r, zl, y2, pl.ds(16, 16)])

    def hid_forward(r, which):
        hidden = zl if which == 0 else 1 - zl
        k = 4 * r + 2 * which
        arrived("hs", k)
        low = gh.at[r, hidden, y1, pl.ds(0, 16)]
        copy("hf", k, low, low, at_y(3))
        arrived("hs", k + 1)
        high = gh.at[r, hidden, y3, pl.ds(16, 16)]
        copy("hf", k + 1, high, high, at_y(1))
        if r in HID_CROSS:
            hid_pair_send(r, 1, gh.at[r, hidden, y1])
            hid_pair_send(r, 2, gh.at[r, hidden, y3])

    def out_product(r):
        arrived("af", 2 * r)
        arrived("af", 2 * r + 1)
        for name in ("ga", "gb", "gc"):
            for side in range(2):
                left(name, 2 * r + side)
        lhs = act[r].reshape(128, 1536)
        g[r] = jnp.dot(lhs, w2[...], preferred_element_type=F32).astype(BF16)
        if r:
            copy("ox", r - 1, g.at[r], orx.at[r - 1], at_x(OFFSET[r]))

    def out_sum():
        for r in range(1, 4):
            arrived("ox", r - 1)
        total = g[0].astype(F32) + orx[0].astype(F32) + orx[1].astype(F32) + orx[2].astype(F32)
        osum[...] = total.astype(BF16).reshape(4, 32, 1536)
        for d in range(1, 4):
            copy("oz", d - 1, osum.at[lax.rem(z + d, 4)], orz.at[d - 1], at_z(d))

    def out_final():
        for d in range(1, 4):
            arrived("oz", d - 1)
        total = osum[z].astype(F32) + orz[0].astype(F32) + orz[1].astype(F32) + orz[2].astype(F32)
        out_ref[...] = total.astype(BF16)

    def second_part(whose):
        core_rows = pl.ds(pl.multiple_of((c if whose else 1 - c) * 768, 256), 768)
        lhs = actt[core_rows]
        for t in range(3):
            cols = pl.ds(t * 512, 512)
            rhs = cotg[:, :, :, cols].reshape(512, 512)
            total = jnp.dot(lhs, rhs, preferred_element_type=F32)
            if whose:
                sg_ref[:, cols] = (total + sgr[:, :, cols].reshape(768, 512).astype(F32)).astype(BF16)
            else:
                for part in range(2):
                    gone[part, :, cols] = total[part * 384 : part * 384 + 384].astype(BF16)

    def second_grad():
        for r in range(4):
            actt[:, pl.ds(r * 128, 128)] = act[r].reshape(128, 1536).T
        second_part(0)
        copy("sg", 0, gone, sgr, core)

    def second_grad_own():
        arrived("sg", 0)
        second_part(1)
        left("sg", 0)

    def in_product(r):
        if r in HID_CROSS:
            for k in range(5):
                arrived("hz", 5 * r + k)
        else:
            for k in range(4):
                arrived("hf", 4 * r + k)
        first = gh[r, 0].reshape(128, 1536)
        second = gh[r, 1].reshape(128, 1536)
        total = jnp.dot(first, wt[0], preferred_element_type=F32)
        total += jnp.dot(second, wt[1], preferred_element_type=F32)
        ig[r] = total.astype(BF16)
        if r:
            copy("ix", r - 1, ig.at[r], irx.at[r - 1], at_x(OFFSET[r]))

    def in_sum():
        for r in range(1, 4):
            arrived("ix", r - 1)
        total = ig[0].astype(F32) + irx[0].astype(F32) + irx[1].astype(F32) + irx[2].astype(F32)
        isum[...] = total.astype(BF16).reshape(4, 32, 768)
        for d in range(1, 4):
            copy("iz", d - 1, isum.at[lax.rem(z + d, 4)], irz.at[d - 1], at_z(d))

    def in_final():
        for d in range(1, 4):
            arrived("iz", d - 1)
        ig_ref[:, own_half] = (isum[z].astype(F32) + irz[1].astype(F32)).astype(BF16)
        ig_ref[:, other_half] = (irz[0].astype(F32) + irz[2].astype(F32)).astype(BF16)

    def transpose_in():
        for r in range(4):
            xgt[:, pl.ds(r * 128, 128)] = xg[r].reshape(128, 768).T

    def transpose_first():
        @pl.loop(0, 6)
        def _(t):
            cols = pl.ds(pl.multiple_of(t * 512, 512), 512)
            spot = pl.ds(pl.multiple_of(lax.rem(t, 3) * 512, 512), 512)
            wt[t // 3, spot] = w1[:, cols].T

    def transpose_second():
        @pl.loop(0, 6)
        def _(t):
            cols = pl.ds(pl.multiple_of(lax.rem(t, 3) * 512, 512), 512)
            some = pl.ds(pl.multiple_of(t // 3 * 768, 768), 768)
            wt[t // 3, cols] = w2[some, cols].T

    def first_grad(half, whose, early):
        core_rows = pl.ds(pl.multiple_of((c if whose else 1 - c) * 384, 128), 384)
        depth = 384 if early else 128
        lhs = xgt[core_rows, pl.ds(128 if early else 0, depth)]
        slots = pl.ds(1, 3) if early else pl.ds(0, 1)
        if whose and not early:
            arrived("fg", half)

        wide = pl.ds(half * 1536, 1536)
        some = gh[slots, half].reshape(depth, 1536)
        total = jnp.dot(lhs, some, preferred_element_type=F32)
        if whose:
            if not early:
                total += fg_ref[:, wide].astype(F32) + fgr[half].astype(F32)
            fg_ref[:, wide] = total.astype(BF16)
        else:
            if not early:
                total += gone[half].astype(F32)
            gone[half] = total.astype(BF16)

        if not whose and not early:
            copy("fg", half, gone.at[half], fgr.at[half], core)

    pre_product(0)
    pass_on("xx", "xf", xg, 0)
    pre_product(2)
    pass_on("xx", "xf", xg, 1)
    pre_product(3)
    pre_forward(0)
    load_cot.wait()
    for k in range(3):
        arrived("cz", k)
    spread("cx", cotg)
    load_w2.wait()
    arrived("w2", 0)
    transpose_second()
    arrived("xf", 0)
    arrived("xf", 1)
    grad_product(0)
    pre_product(1)
    pre_forward(3)
    pre_cross(2)
    pass_on("cx", "cf", cotg, 0)
    grad_product(2)
    pass_on("cx", "cf", cotg, 1)
    pre_forward(2)
    grad_product(3)
    grad_forward(2)
    pre_cross(1)
    pre_sum(3)
    pre_sum(0)
    arrived("cf", 0)
    arrived("cf", 1)
    pre_sum(2)
    gelu(2)
    grad_product(1)
    pre_forward(1)
    gelu(3)
    hidden_grad(2)
    transpose_first()
    grad_forward(1)
    pre_sum(1)
    gelu(1)
    act_send(1)
    act_send(3)
    hid_forward(2, 0)
    act_forward(1)
    hidden_grad(1)
    act_send(2)
    gelu(0)
    hid_rest(2)
    out_product(1)
    grad_forward(3)
    hid_forward(1, 0)
    act_forward(2)
    act_forward(3)
    grad_forward(0)
    hid_rest(1)
    hidden_grad(3)
    act_send(0)
    out_product(2)
    out_product(3)
    hidden_grad(0)
    hid_forward(3, 0)
    in_product(1)
    act_forward(0)
    in_product(2)
    hidden_pair(0)
    hid_rest(3)
    hid_forward(0, 0)
    transpose_in()
    out_product(0)
    second_grad()
    hid_forward(0, 1)
    in_product(3)
    out_sum()
    in_product(0)
    second_grad_own()
    for half in range(2):
        first_grad(half, 0, True)
    in_sum()
    for half in range(2):
        first_grad(half, 0, False)
    for half in range(2):
        first_grad(half, 1, True)
    out_final()
    for half in range(2):
        first_grad(half, 1, False)
    in_final()
    for made in sent.values():
        made.wait_send()


def leave(*refs):
    sems = refs[-1]
    copies = [pltpu.make_async_copy(refs[i], refs[4 + i], sems.at[i]) for i in range(4)]
    for made in copies:
        made.start()
    for made in copies:
        made.wait()


def shards(inputs, first_weight, second_weight, cotangent):
    def vmem(*shape, dtype=BF16):
        return pltpu.VMEM(shape, dtype)

    anywhere = pl.BlockSpec(memory_space=pl.ANY)
    inside = pl.BlockSpec(memory_space=pltpu.VMEM)
    shapes = [(32, 1536), (32, 1536), (384, 3072), (768, 1536)]
    results = pl.pallas_call(
        kernel,
        out_shape=[pltpu.VMEM(shape, BF16) for shape in shapes],
        in_specs=[anywhere] * 4,
        out_specs=[inside] * 4,
        scratch_shapes=[
            vmem(768, 3072), vmem(1536, 1536), vmem(2, 1536, 768), vmem(4, 4, 32, 768), vmem(768, 512), vmem(4, 4, 32, 1536),
            vmem(4, 2, 128, 1536), vmem(4, 2, 2, 16, 1536), vmem(4, 2, 2, 16, 1536), vmem(4, 2, 2, 16, 1536),
            vmem(4, 32, 1536), vmem(4, 32, 1536), vmem(len(PRE_CROSS), 128, 1536),
            vmem(4, 128, 1536), vmem(4, 2, 16, 1536), vmem(4, 2, 16, 1536), vmem(4, 2, 16, 1536),
            vmem(4, 32, 1536, dtype=F32), vmem(4, 4, 32, 1536), vmem(1536, 512), vmem(4, 2, 4, 32, 1536),
            vmem(3, 128, 1536), vmem(4, 32, 1536), vmem(3, 32, 1536),
            vmem(4, 128, 768), vmem(3, 128, 768), vmem(4, 32, 768), vmem(3, 32, 768),
            vmem(2, 384, 1536), vmem(2, 384, 1536), vmem(2, 384, 1536),
            pltpu.SemaphoreType.DMA((N_MESSAGES,)),
            pltpu.SemaphoreType.DMA((N_MESSAGES,)),
            pltpu.SemaphoreType.DMA((4,)),
        ],
        compiler_params=pltpu.CompilerParams(
            collective_id=0, has_side_effects=True, vmem_limit_bytes=50 << 20
        ),
        name="layer",
    )(inputs, first_weight, second_weight, cotangent)
    results = [pltpu.with_memory_space_constraint(result, pltpu.VMEM) for result in results]
    return pl.pallas_call(
        leave,
        out_shape=[jax.ShapeDtypeStruct(shape, BF16) for shape in shapes],
        in_specs=[inside] * 4,
        out_specs=[anywhere] * 4,
        scratch_shapes=[pltpu.SemaphoreType.DMA((4,))],
        compiler_params=pltpu.CompilerParams(vmem_limit_bytes=1 << 20),
        name="leave",
    )(*results)


def solution(mesh):
    in_specs = (
        P(("ia", "al"), "ja"),
        P(("ja", "ia"), "al"),
        P(("al", "ia"), "ja"),
        P(("ia", "al"), "ja"),
    )
    out_specs = (
        P(("ia", "al"), "ja"),
        P(("ia", "al"), "ja"),
        P(("ja", "ia"), "al"),
        P(("al", "ia"), "ja"),
    )
    return jax.shard_map(shards, mesh=mesh, in_specs=in_specs, out_specs=out_specs, check_vma=False)
```
